128 devices in a mesh: dp: 16 (over x_hi, y, core), tensor: 8 (over z, x_lo).
Axes of the slice: x: 4 (x_hi: 2, x_lo: 2; x = x_hi * 2 + x_lo), y: 4, z: 4, core: 2. Of those that a mesh axis runs over, the one named last changes fastest.
Arguments:
- hidden_in: bfloat16 [16384, 1024], P(('dp', 'tensor')), may hold values from -6 to 6
- segment_ids: int32 [16384], P(('dp', 'tensor')), may hold values from -1 to 129, as said below
- w_qkv: bfloat16 [2, 1024, 3, 1024], P(None, 'dp', None, 'tensor'), may hold values from -0.1875 to 0.1875
- b_qv: float32 [2, 2, 1024], P(None, None, 'tensor'), may hold values from -3 to 3
- w_out: bfloat16 [2, 1024, 1024], P(None, 'tensor', 'dp'), may hold values from -1.5 to 1.5
- b_out: float32 [2, 1024], replicated, may hold values from -2 to 2
- ln1_gain: float32 [2, 1024], replicated, may hold values from 0.5 to 1.5
- ln1_bias: float32 [2, 1024], replicated, may hold values from -2 to 2
- w_up: bfloat16 [2, 1024, 4096], P(None, 'dp', 'tensor'), may hold values from -0.1875 to 0.1875
- b_up: float32 [2, 4096], P(None, 'tensor'), may hold values from -3 to 3
- w_down: bfloat16 [2, 4096, 1024], P(None, 'tensor', 'dp'), may hold values from -0.125 to 0.125
- b_down: float32 [2, 1024], replicated, may hold values from -2 to 2
- ln2_gain: float32 [2, 1024], replicated, may hold values from 0.5 to 1.5
- ln2_bias: float32 [2, 1024], replicated, may hold values from -2 to 2
- out_grad: bfloat16 [16384, 1024], P(('dp', 'tensor')), may hold values from -6 to 6
Outputs:
- hidden_out: bfloat16 [16384, 1024], P(('dp', 'tensor'))
- hidden_grad: float32 [16384, 1024], P(('dp', 'tensor'))
- grad_w_qkv: float32 [2, 1024, 3, 1024], P(None, 'dp', None, 'tensor')
- grad_b_qv: float32 [2, 2, 1024], P(None, None, 'tensor')
- grad_w_out: float32 [2, 1024, 1024], P(None, 'tensor', 'dp')
- grad_b_out: float32 [2, 1024], replicated
- grad_ln1_gain: float32 [2, 1024], replicated
- grad_ln1_bias: float32 [2, 1024], replicated
- grad_w_up: float32 [2, 1024, 4096], P(None, 'dp', 'tensor')
- grad_b_up: float32 [2, 4096], P(None, 'tensor')
- grad_w_down: float32 [2, 4096, 1024], P(None, 'tensor', 'dp')
- grad_b_down: float32 [2, 1024], replicated
- grad_ln2_gain: float32 [2, 1024], replicated
- grad_ln2_bias: float32 [2, 1024], replicated
The draws below stay inside these ranges and needn't reach their ends.
Inputs may be any that keep to these rules, and one draw needn't show every extreme that they name: `segment_ids`: in each group of 1024 slots: zero or more short documents, then one document with id 128 + 1 that starts within the group's first 128 slots and ends within its last 128 slots, then one or more empty slots (-1). Document ids are compared only for equality.
All inputs are finite; a program needn't handle non-finite values.
Results may differ from the reference program's by a relative error of at most 0.023.
Values may be sent and summed in bfloat16 or wider, within the bound.
No kernel may reach another device: no remote copies, remote signals or barrier semaphores. Data moves between devices by JAX's collectives and lax.ppermute only.
A program may use at most 128 MiB of HBM per device.

```python
import jax
import jax.numpy as jnp
from jax import lax

HEADS = 16
HEAD_DIM = 64
FF = 4096
LAYERS = 2
D = 1024
GROUP = 1024
ROWS = 128
TOKENS = 16384
N_DP = 16
N_TENSOR = 8


def draw_segment_ids(key, part):
    key = jax.random.fold_in(key, 7)

    def one_group(group_key):
        key_start, key_end, key_flags = jax.random.split(group_key, 3)
        main_start = jax.random.randint(key_start, (), 0, ROWS)
        main_end = jax.random.randint(key_end, (), GROUP - ROWS + 1, GROUP)
        flags = (jax.random.randint(key_flags, (GROUP,), 0, 8) == 0).astype(jnp.int32)
        short_ids = jnp.cumsum(flags) + 1
        positions = jnp.arange(GROUP).astype(jnp.int32)
        return jnp.where(positions < main_start, short_ids, jnp.where(positions < main_end, ROWS + 1, -1)).astype(jnp.int32)
    group_keys = jax.random.split(key, N_DP)
    return jax.vmap(one_group)(group_keys).reshape(-1)


def levels(key, extent, shards, low, top_value):
    loudness, own = 1.0, jax.random.fold_in(key, 6)
    for axis_at, shards_of in shards:
        heights = jnp.exp(jax.random.uniform(jax.random.fold_in(own, axis_at), (shards_of,), jnp.float32, low / len(shards), top_value / len(shards)))
        loudness = loudness * jnp.repeat(heights, extent[axis_at] // shards_of).reshape([-1 if axis == axis_at else 1 for axis in range(len(extent))])
    return loudness


def noise(key, shape, width, reach, cuts=(), kind=jnp.bfloat16):
    entries = width * jax.random.normal(key, shape, jnp.float32)
    if cuts:
        entries = entries * levels(key, shape, cuts, -0.22, 0.18)
    return jnp.clip(entries, -reach, reach).astype(kind)


def setup_inputs(seed: int = 0) -> dict:
    key_list = jax.random.split(jax.random.key(seed), 16)
    return {
        "hidden_in": noise(key_list[0], (TOKENS, D), 1.0, 6.0, ((0, 128),)),
        "segment_ids": draw_segment_ids(jax.random.fold_in(key_list[15], 71), 0),
        "w_qkv": noise(key_list[2], (LAYERS, D, 3, D), D ** -0.5, 0.1875, ((1, 16), (3, 8))),
        "b_qv": noise(key_list[3], (LAYERS, 2, D), 0.5, 3.0, ((2, 8),), jnp.float32),
        "w_out": noise(key_list[4], (LAYERS, D, D), (D // 64) ** -0.5, 1.5, ((1, 8), (2, 16))),
        "b_out": noise(key_list[5], (LAYERS, D), 0.3, 2.0, (), jnp.float32),
        "ln1_gain": jnp.clip(1.0 + 0.1 * jax.random.normal(key_list[6], (LAYERS, D), jnp.float32), 0.5, 1.5),
        "ln1_bias": noise(key_list[7], (LAYERS, D), 0.3, 2.0, (), jnp.float32),
        "w_up": noise(key_list[8], (LAYERS, D, FF), D ** -0.5, 0.1875, ((1, 16), (2, 8))),
        "b_up": noise(key_list[9], (LAYERS, FF), 0.5, 3.0, ((1, 8),), jnp.float32),
        "w_down": noise(key_list[10], (LAYERS, FF, D), (FF // 2) ** -0.5, 0.125, ((1, 8), (2, 16))),
        "b_down": noise(key_list[11], (LAYERS, D), 0.3, 2.0, (), jnp.float32),
        "ln2_gain": jnp.clip(1.0 + 0.1 * jax.random.normal(key_list[12], (LAYERS, D), jnp.float32), 0.5, 1.5),
        "ln2_bias": noise(key_list[13], (LAYERS, D), 0.3, 2.0, (), jnp.float32),
        "out_grad": noise(key_list[14], (TOKENS, D), 1.0, 6.0, ((0, 128),)),
    }


@jax.custom_vjp
def low(v):
    return lax.optimization_barrier(v.astype(jnp.bfloat16)).astype(jnp.float32)

@jax.custom_vjp
def low_back(v):
    return v

def low_keep(v):
    return (low(v), None)

def low_pass(kept, grad):
    return (grad,)

def back_keep(v):
    return (v, None)

def back_low(kept, grad):
    return (low(grad),)
low.defvjp(low_keep, low_pass)
low_back.defvjp(back_keep, back_low)
eps = 1e-05
big_negative = -1e+30
HIGH = lax.Precision.HIGHEST

def norm_rows(values, scale_vec, shift_vec):
    center = values - lax.optimization_barrier(jnp.mean(values, axis=-1, keepdims=True))
    spread = lax.optimization_barrier(jnp.mean(center * center, axis=-1, keepdims=True))
    return center * lax.rsqrt(spread + eps) * scale_vec + shift_vec

def run_group(hidden, seg, params):
    w_qkv, b_qv, w_out, b_out, ln1_gain, ln1_bias, w_up, b_up, w_down, b_down, ln2_gain, ln2_bias = params
    positions = jnp.arange(GROUP).astype(jnp.int32)
    allowed = (seg[:, None] == seg[None, :]) & (seg[:, None] >= 0) & (positions[None, :] <= positions[:, None]) | (positions[:, None] == positions[None, :])
    head_cols = D // N_TENSOR
    unit_cols = FF // N_TENSOR
    score_scale = HEAD_DIM ** (-0.5)
    for layer_at in range(LAYERS):
        normed = low(norm_rows(hidden, ln1_gain[layer_at], ln1_bias[layer_at]))
        pre_qkv = jnp.dot(normed, w_qkv[layer_at].reshape(D, 3 * D), precision=HIGH).reshape(GROUP, 3, D)
        qkv_bias = jnp.stack([b_qv[layer_at, 0], jnp.zeros_like(b_qv[layer_at, 0]), b_qv[layer_at, 1]])
        qkv = low(low_back(pre_qkv + qkv_bias[None]))
        queries = qkv[:, 0].reshape(GROUP, HEADS, HEAD_DIM)
        keys_all = qkv[:, 1].reshape(GROUP, HEADS, HEAD_DIM)
        values_all = qkv[:, 2].reshape(GROUP, HEADS, HEAD_DIM)
        scores = jnp.einsum('qhd,khd->hqk', queries, keys_all, precision=HIGH) * score_scale
        scores = low_back(jnp.where(allowed[None], scores, big_negative))
        row_top = lax.optimization_barrier(jnp.max(scores, axis=-1, keepdims=True))
        expo = jnp.exp(scores - row_top)
        attn_prob = expo / lax.optimization_barrier(jnp.sum(expo, axis=-1, keepdims=True))
        mixed = jnp.einsum('hqk,khd->qhd', low(attn_prob), values_all, precision=HIGH).reshape(GROUP, D)
        mixed = low(low_back(mixed))
        partials = jnp.einsum('gtc,tce->tge', mixed.reshape(GROUP, N_TENSOR, head_cols), w_out[layer_at].reshape(N_TENSOR, head_cols, D), precision=HIGH)
        hidden = hidden + low_back(lax.optimization_barrier(jnp.sum(low(partials), axis=0)) + b_out[layer_at])
        cnorm = low(norm_rows(hidden, ln2_gain[layer_at], ln2_bias[layer_at]))
        pre_up = low_back(jnp.dot(cnorm, w_up[layer_at], precision=HIGH) + b_up[layer_at])
        act_lo = low(jax.nn.gelu(pre_up, approximate=True))
        partials = jnp.einsum('gtf,tfe->tge', act_lo.reshape(GROUP, N_TENSOR, unit_cols), w_down[layer_at].reshape(N_TENSOR, unit_cols, D), precision=HIGH)
        hidden = hidden + low_back(lax.optimization_barrier(jnp.sum(low(partials), axis=0)) + b_down[layer_at])
    return hidden

def reference(hidden_in, segment_ids, w_qkv, b_qv, w_out, b_out, ln1_gain, ln1_bias, w_up, b_up, w_down, b_down, ln2_gain, ln2_bias, out_grad):
    params = tuple((item.astype(jnp.float32) for item in (w_qkv, b_qv, w_out, b_out, ln1_gain, ln1_bias, w_up, b_up, w_down, b_down, ln2_gain, ln2_bias)))
    start_rows = hidden_in.astype(jnp.float32).reshape(N_DP, GROUP, D)
    segs = segment_ids.reshape(N_DP, GROUP)

    def forward(start_rows, params):
        step_fn = jax.checkpoint(run_group)

        def scan_fn(carry, inputs):
            return (carry, step_fn(inputs[0], inputs[1], params))
        _, end_rows = lax.scan(scan_fn, None, (start_rows, segs))
        return end_rows
    end_rows, pull_back = jax.vjp(forward, start_rows, params)
    grad_rows, grads = pull_back(out_grad.astype(jnp.float32).reshape(N_DP, GROUP, D))
    return (end_rows.reshape(TOKENS, D).astype(jnp.bfloat16), grad_rows.reshape(TOKENS, D), grads[0], grads[1], grads[2], grads[3], grads[4], grads[5], grads[6], grads[7], grads[8], grads[9], grads[10], grads[11])
```

```python
import jax
import jax.numpy as jnp
from jax import lax
from jax.experimental import pallas as pl
from jax.experimental.pallas import tpu as pltpu
from jax.sharding import Mesh
from jax.sharding import PartitionSpec as P

HEAD_DIM = 64
eps = 1e-05
big_negative = -1e30
score_scale = HEAD_DIM ** (-0.5)

AXES = ("xh", "y", "c", "z", "xl")
PLANE = ("xh", "y", "xl")
PLANE_CORES = ("xh", "y", "xl", "c")
CHUNK = 128


def norm_rows(values, scale_vec, shift_vec):
    center = values - jnp.mean(values, axis=-1, keepdims=True)
    spread = jnp.mean(center * center, axis=-1, keepdims=True)
    return center * lax.rsqrt(spread + eps) * scale_vec + shift_vec


def gelu_tanh(values):
    return jax.nn.gelu(values, approximate=True)


def swap_rows(values):
    return lax.ppermute(values, ("c", "xl"), [(0, 0), (1, 2), (2, 1), (3, 3)])


def other_core(values):
    return lax.ppermute(values, "c", [(0, 1), (1, 0)])


def share(values, axis, count):
    copies = jnp.broadcast_to(values[None], (count,) + values.shape)
    return lax.all_to_all(copies, axis, 0, 0, tiled=True)


def spread_z(rows):
    return share(rows, "z", 4).reshape(4 * rows.shape[0], rows.shape[1])


def collect_z(partials):
    low = partials.astype(jnp.bfloat16)
    chunks = low.reshape(4, low.shape[0] // 4, low.shape[1])
    arrived = lax.all_to_all(chunks, "z", 0, 0, tiled=True)
    return jnp.sum(arrived.astype(jnp.float32), axis=0)


def nt_dot(left, right):
    return lax.dot_general(left, right, (((1,), (1,)), ((), ())), preferred_element_type=jnp.float32)


def nn_dot(left, right):
    return jnp.dot(left, right, preferred_element_type=jnp.float32)


def interleave(own, other):
    pieces = []
    for at in range(own.shape[0] // CHUNK):
        pieces += [own[at * CHUNK : (at + 1) * CHUNK], other[at * CHUNK : (at + 1) * CHUNK]]
    return jnp.concatenate(pieces, axis=0)


def by_head(block):
    first = lax.broadcasted_iota(jnp.int32, block.shape, 1) < HEAD_DIM
    zero = jnp.zeros_like(block)
    return jnp.concatenate([jnp.where(first, block, zero), jnp.where(first, zero, block)], axis=0)


def pick_heads(both):
    first = lax.broadcasted_iota(jnp.int32, (CHUNK, CHUNK), 0) < HEAD_DIM
    return jnp.where(first, both[:, :CHUNK], both[:, CHUNK:]).T


def tile_mask(keys_ref, rows_ref, at):
    key_count = 2 * CHUNK * (at + 1)
    seg_keys, pos_keys = keys_ref[0, :key_count], keys_ref[1, :key_count]
    seg_rows = rows_ref[0:1, at * CHUNK : (at + 1) * CHUNK]
    pos_rows = rows_ref[1:2, at * CHUNK : (at + 1) * CHUNK]
    allowed = ((seg_keys == seg_rows) & (seg_rows >= 0) & (pos_keys <= pos_rows)) | (
        pos_keys == pos_rows
    )
    bias = jnp.where(allowed, 0.0, big_negative)
    return jnp.concatenate([bias, bias], axis=1)


def masked_scores(keys_all, q_heads, bias):
    scores = nt_dot(keys_all, q_heads) * score_scale
    return jnp.where(bias < 0.0, big_negative, scores)


def forward_kernel(qkv_ref, kv_ref, keys_ref, rows_ref, mixed_ref, lse_ref):
    tiles = qkv_ref.shape[0] // CHUNK
    biases = [tile_mask(keys_ref, rows_ref, at) for at in range(tiles)]
    for block in range(2):
        base = block * 3 * CHUNK
        k_own = qkv_ref[:, base + CHUNK : base + 2 * CHUNK]
        v_own = qkv_ref[:, base + 2 * CHUNK : base + 3 * CHUNK]
        k_other = kv_ref[:, block * 2 * CHUNK : block * 2 * CHUNK + CHUNK]
        v_other = kv_ref[:, block * 2 * CHUNK + CHUNK : block * 2 * CHUNK + 2 * CHUNK]
        keys_all = interleave(k_own, k_other)
        values_t = interleave(v_own, v_other).T
        for at in range(tiles):
            rows = slice(at * CHUNK, (at + 1) * CHUNK)
            count = 2 * CHUNK * (at + 1)
            q_heads = by_head(qkv_ref[rows, base : base + CHUNK])
            scores = masked_scores(keys_all[:count], q_heads, biases[at])
            top = jnp.max(scores, axis=0, keepdims=True)
            expo = jnp.exp(scores - top)
            total = jnp.sum(expo, axis=0, keepdims=True)
            prob = (expo * (1.0 / total)).astype(jnp.bfloat16)
            mixed = pick_heads(nn_dot(values_t[:, :count], prob))
            mixed_ref[rows, block * CHUNK : (block + 1) * CHUNK] = mixed.astype(jnp.bfloat16)
            lse = top + jnp.log(total)
            lse_ref[2 * block : 2 * block + 1, rows] = lse[:, :CHUNK]
            lse_ref[2 * block + 1 : 2 * block + 2, rows] = lse[:, CHUNK:]


def backward_kernel(
    qkv_ref, kv_ref, keys_ref, rows_ref, lse_ref, dmix_ref, dq_ref, own_ref, other_ref, dk_ref, dv_ref
):
    tiles = qkv_ref.shape[0] // CHUNK
    biases = [tile_mask(keys_ref, rows_ref, at) for at in range(tiles)]
    for block in range(2):
        base = block * 3 * CHUNK
        k_own = qkv_ref[:, base + CHUNK : base + 2 * CHUNK]
        v_own = qkv_ref[:, base + 2 * CHUNK : base + 3 * CHUNK]
        k_other = kv_ref[:, block * 2 * CHUNK : block * 2 * CHUNK + CHUNK]
        v_other = kv_ref[:, block * 2 * CHUNK + CHUNK : block * 2 * CHUNK + 2 * CHUNK]
        keys_all = interleave(k_own, k_other)
        values_all = interleave(v_own, v_other)
        keys_t = keys_all.T
        for at in reversed(range(tiles)):
            rows = slice(at * CHUNK, (at + 1) * CHUNK)
            count = 2 * CHUNK * (at + 1)
            q_heads = by_head(qkv_ref[rows, base : base + CHUNK])
            dm_heads = by_head(dmix_ref[rows, block * CHUNK : (block + 1) * CHUNK])
            lse = jnp.concatenate(
                [lse_ref[2 * block : 2 * block + 1, rows], lse_ref[2 * block + 1 : 2 * block + 2, rows]],
                axis=1,
            )
            scores = masked_scores(keys_all[:count], q_heads, biases[at])
            prob = jnp.exp(scores - lse)
            dprob = nt_dot(values_all[:count], dm_heads)
            weighted = jnp.sum(prob * dprob, axis=0, keepdims=True)
            dscore = (prob * (dprob - weighted)).astype(jnp.bfloat16)
            prob_low = prob.astype(jnp.bfloat16)
            dq = pick_heads(nn_dot(keys_t[:, :count], dscore)) * score_scale
            dq_ref[rows, block * CHUNK : (block + 1) * CHUNK] = dq.astype(jnp.bfloat16)
            dk = nn_dot(dscore, q_heads) * score_scale
            dv = nn_dot(prob_low, dm_heads)
            if at == tiles - 1:
                dk_ref[...] = dk
                dv_ref[...] = dv
            else:
                dk_ref[:count] += dk
                dv_ref[:count] += dv
        for at in range(tiles):
            rows = slice(at * CHUNK, (at + 1) * CHUNK)
            mine = slice(2 * at * CHUNK, (2 * at + 1) * CHUNK)
            theirs = slice((2 * at + 1) * CHUNK, (2 * at + 2) * CHUNK)
            k_cols = slice(block * 2 * CHUNK, block * 2 * CHUNK + CHUNK)
            v_cols = slice(block * 2 * CHUNK + CHUNK, block * 2 * CHUNK + 2 * CHUNK)
            own_ref[rows, k_cols] = dk_ref[mine]
            own_ref[rows, v_cols] = dv_ref[mine]
            other_ref[rows, k_cols] = dk_ref[theirs].astype(jnp.bfloat16)
            other_ref[rows, v_cols] = dv_ref[theirs].astype(jnp.bfloat16)


def whole(count):
    return [pl.BlockSpec(memory_space=pltpu.VMEM)] * count


def attend_forward(qkv, kv_other, keys_info, rows_info):
    rows = qkv.shape[0]
    return pl.pallas_call(
        forward_kernel,
        out_shape=(
            jax.ShapeDtypeStruct((rows, 2 * CHUNK), jnp.bfloat16),
            jax.ShapeDtypeStruct((8, rows), jnp.float32),
        ),
        in_specs=whole(4),
        out_specs=tuple(whole(2)),
        compiler_params=pltpu.CompilerParams(vmem_limit_bytes=40 * 1024 * 1024),
        cost_estimate=pl.CostEstimate(flops=700_000_000, bytes_accessed=4_000_000, transcendentals=1_400_000),
        name="attend_forward",
    )(qkv, kv_other, keys_info, rows_info)


def attend_backward(qkv, kv_other, keys_info, rows_info, lse, dmix):
    rows = qkv.shape[0]
    return pl.pallas_call(
        backward_kernel,
        out_shape=(
            jax.ShapeDtypeStruct((rows, 2 * CHUNK), jnp.bfloat16),
            jax.ShapeDtypeStruct((rows, 4 * CHUNK), jnp.float32),
            jax.ShapeDtypeStruct((rows, 4 * CHUNK), jnp.bfloat16),
        ),
        in_specs=whole(6),
        out_specs=tuple(whole(3)),
        scratch_shapes=[
            pltpu.VMEM((2 * rows, CHUNK), jnp.float32),
            pltpu.VMEM((2 * rows, CHUNK), jnp.float32),
        ],
        compiler_params=pltpu.CompilerParams(vmem_limit_bytes=40 * 1024 * 1024),
        cost_estimate=pl.CostEstimate(flops=1_700_000_000, bytes_accessed=6_000_000, transcendentals=1_400_000),
        name="attend_backward",
    )(qkv, kv_other, keys_info, rows_info, lse, dmix)


def quarter(own, other, core):
    slabs, depth, cols = own.shape
    first = core == 0
    own = own.reshape(slabs // 2, 2, depth, cols)
    other = other.reshape(slabs // 2, 2, depth, cols)
    pair = jnp.stack([jnp.where(first, own, other), jnp.where(first, other, own)], axis=1)
    return pair.transpose(0, 1, 3, 2, 4).reshape(slabs * depth, 2, cols)


def core_sum(grad, core):
    depth = 64
    cols = grad.shape[2]
    low = grad.astype(jnp.bfloat16).reshape(8, 2, depth, 2, cols)
    keep = lax.dynamic_index_in_dim(low, core, 1, False).transpose(0, 2, 1, 3)
    give = lax.dynamic_index_in_dim(low, 1 - core, 1, False).transpose(0, 2, 1, 3)
    both = keep.astype(jnp.float32) + other_core(give).astype(jnp.float32)
    return both.astype(jnp.bfloat16).reshape(16, depth, cols)


def norm_pullback(values, gain, shift, grad):
    _, pull = jax.vjp(norm_rows, values, gain, shift)
    return pull(grad)


def local(
    hidden_in,
    segment_ids,
    w_qkv,
    b_qv,
    w_out,
    b_out,
    ln1_gain,
    ln1_bias,
    w_up,
    b_up,
    w_down,
    b_down,
    ln2_gain,
    ln2_bias,
    out_grad,
):
    layer_count = w_qkv.shape[0]
    core = lax.axis_index("c")
    lane = lax.axis_index("xl")

    resid = swap_rows(hidden_in).astype(jnp.float32)

    attn_slab = [
        jnp.concatenate([w_qkv[at].reshape(64, 3 * CHUNK), w_out[at].T], axis=1)
        for at in range(layer_count)
    ]
    feed_slab = [jnp.concatenate([w_up[at], w_down[at].T], axis=1) for at in range(layer_count)]

    def plane_share(slab):
        return share(slab, PLANE, 16)

    def plane_gather(slab):
        return lax.all_gather(slab, PLANE, axis=0)

    gathered_attn = [plane_share(attn_slab[0])]
    gathered_feed = [plane_share(feed_slab[0])]
    later = plane_gather(jnp.concatenate([attn_slab[1], feed_slab[1]], axis=1))
    gathered_attn.append(later[..., : 4 * CHUNK])
    gathered_feed.append(later[..., 4 * CHUNK :])

    seg_pairs = share(segment_ids[None], ("c", "z", "xl"), 16).reshape(2, 4, 2, CHUNK)
    seg_pairs = lax.dynamic_index_in_dim(seg_pairs, lane, 0, False)
    seg_own = lax.dynamic_index_in_dim(seg_pairs, core, 1, False)
    seg_other = lax.dynamic_index_in_dim(seg_pairs, 1 - core, 1, False)
    spots = lax.broadcasted_iota(jnp.int32, (4, CHUNK), 0) * (2 * CHUNK) + lax.broadcasted_iota(
        jnp.int32, (4, CHUNK), 1
    )
    pos_own = spots + core * CHUNK
    pos_other = spots + (1 - core) * CHUNK
    rows_info = jnp.stack([seg_own.reshape(-1), pos_own.reshape(-1)])
    rows_info = jnp.concatenate([rows_info, jnp.zeros((6, 4 * CHUNK), jnp.int32)], axis=0)
    seg_keys = jnp.stack([seg_own, seg_other], axis=1).reshape(8 * CHUNK, 1)
    pos_keys = jnp.stack([pos_own, pos_other], axis=1).reshape(8 * CHUNK, 1)
    keys_info = jnp.broadcast_to(jnp.stack([seg_keys, pos_keys]), (2, 8 * CHUNK, CHUNK))

    bias_mine = jnp.concatenate([b_qv.reshape(layer_count, 2 * CHUNK), b_up], axis=1)
    bias_next = lax.ppermute(bias_mine, "xl", [(0, 1), (1, 0)])
    bias_both = jnp.stack(
        [jnp.where(lane == 0, bias_mine, bias_next), jnp.where(lane == 0, bias_next, bias_mine)], axis=1
    )

    saved = []
    weights = []
    for at in range(layer_count):
        attn_w = quarter(gathered_attn[at], other_core(gathered_attn[at]), core)
        feed_w = quarter(gathered_feed[at], other_core(gathered_feed[at]), core)
        wq = attn_w[..., : 3 * CHUNK].reshape(1024, 6 * CHUNK)
        wo_t = attn_w[..., 3 * CHUNK :].reshape(1024, 2 * CHUNK)
        wu = feed_w[..., :512].reshape(1024, 1024)
        wd_t = feed_w[..., 512:].reshape(1024, 1024)
        weights.append((wq, wo_t, wu, wd_t))
        zero = jnp.zeros((2, CHUNK), jnp.float32)
        qkv_bias = jnp.concatenate(
            [bias_both[at][:, :CHUNK], zero, bias_both[at][:, CHUNK : 2 * CHUNK]], axis=1
        ).reshape(6 * CHUNK)
        up_bias = bias_both[at][:, 2 * CHUNK :].reshape(1024)

        normed = norm_rows(resid, ln1_gain[at], ln1_bias[at]).astype(jnp.bfloat16)
        normed_full = spread_z(normed)
        qkv = (nn_dot(normed_full, wq) + qkv_bias).astype(jnp.bfloat16)
        kv_mine = jnp.concatenate([qkv[:, CHUNK : 3 * CHUNK], qkv[:, 4 * CHUNK :]], axis=1)
        kv_other = other_core(kv_mine)
        mixed, lse = attend_forward(qkv, kv_other, keys_info, rows_info)
        branch = collect_z(nt_dot(mixed, wo_t))
        resid_mid = resid + branch + b_out[at]
        cnorm = norm_rows(resid_mid, ln2_gain[at], ln2_bias[at]).astype(jnp.bfloat16)
        cnorm_full = spread_z(cnorm)
        pre_up = nn_dot(cnorm_full, wu) + up_bias
        act = gelu_tanh(pre_up).astype(jnp.bfloat16)
        branch = collect_z(nt_dot(act, wd_t))
        saved.append((resid, normed_full, qkv, kv_other, mixed, lse, resid_mid, cnorm_full, pre_up, act))
        resid = resid_mid + branch + b_down[at]
    hidden_out = swap_rows(resid.astype(jnp.bfloat16))

    grad = swap_rows(out_grad).astype(jnp.float32)
    shared = [None] * layer_count
    units = [None] * layer_count
    attn_out = [None] * layer_count
    feed_out = [None] * layer_count
    for at in reversed(range(layer_count)):
        resid_in, normed_full, qkv, kv_other, mixed, lse, resid_mid, cnorm_full, pre_up, act = saved[at]
        wq, wo_t, wu, wd_t = weights[at]

        low = grad.astype(jnp.bfloat16)
        g_bdown = jnp.sum(low.astype(jnp.float32), axis=0)
        low_full = spread_z(low)
        d_act = nn_dot(low_full, wd_t)
        _, gelu_pull = jax.vjp(gelu_tanh, pre_up)
        d_pre = gelu_pull(d_act)[0].astype(jnp.bfloat16)
        g_bup = jnp.sum(d_pre.astype(jnp.float32), axis=0)
        d_cnorm = collect_z(nt_dot(d_pre, wu))
        g_wdown = lax.dot_general(
            low_full, act, (((0,), (0,)), ((), ())), preferred_element_type=jnp.float32
        )
        g_wup = lax.dot_general(
            cnorm_full, d_pre, (((0,), (0,)), ((), ())), preferred_element_type=jnp.float32
        )
        feed_sum = core_sum(
            jnp.concatenate([g_wup.reshape(1024, 2, 512), g_wdown.reshape(1024, 2, 512)], axis=2), core
        )
        d_x, g_g2, g_s2 = norm_pullback(resid_mid, ln2_gain[at], ln2_bias[at], d_cnorm)
        grad = grad + d_x

        low = grad.astype(jnp.bfloat16)
        g_bout = jnp.sum(low.astype(jnp.float32), axis=0)
        low_full = spread_z(low)
        d_mix = nn_dot(low_full, wo_t).astype(jnp.bfloat16)
        d_q, d_own, d_other = attend_backward(qkv, kv_other, keys_info, rows_info, lse, d_mix)
        d_kv = (d_own + other_core(d_other).astype(jnp.float32)).astype(jnp.bfloat16)
        d_qkv = jnp.concatenate(
            [d_q[:, :CHUNK], d_kv[:, : 2 * CHUNK], d_q[:, CHUNK:], d_kv[:, 2 * CHUNK :]], axis=1
        )
        d_normed = collect_z(nt_dot(d_qkv, wq))
        sums = jnp.sum(d_qkv.astype(jnp.float32), axis=0).reshape(2, 3, CHUNK)
        g_bqv = jnp.stack([sums[:, 0], sums[:, 2]])
        g_wout = lax.dot_general(
            low_full, mixed, (((0,), (0,)), ((), ())), preferred_element_type=jnp.float32
        )
        g_wqkv = lax.dot_general(
            normed_full, d_qkv, (((0,), (0,)), ((), ())), preferred_element_type=jnp.float32
        )
        attn_sum = core_sum(
            jnp.concatenate([g_wqkv.reshape(1024, 2, 384), g_wout.reshape(1024, 2, 128)], axis=2), core
        )
        d_x, g_g1, g_s1 = norm_pullback(resid_in, ln1_gain[at], ln1_bias[at], d_normed)
        grad = grad + d_x

        if at > 0:
            both = lax.psum_scatter(
                jnp.concatenate([attn_sum, feed_sum], axis=2), PLANE, scatter_dimension=0
            ).astype(jnp.float32)
            attn_out[at], feed_out[at] = both[:, : 4 * CHUNK], both[:, 4 * CHUNK :]
        else:
            feed_out[at] = lax.psum_scatter(feed_sum, PLANE, scatter_dimension=0).astype(jnp.float32)
            parts = lax.all_to_all(attn_sum, PLANE, 0, 0, tiled=True)
            attn_out[at] = jnp.sum(parts.astype(jnp.float32), axis=0)
        shared[at] = (g_bout, g_g1, g_s1, g_bdown, g_g2, g_s2)
        units[at] = (g_bqv, g_bup)
    hidden_grad = swap_rows(grad)

    early = jnp.stack([*shared[1], shared[0][0], *shared[0][3:]])
    early = jnp.sum(share(early, "z", 4), axis=0)
    unit_rows = jnp.concatenate(
        [
            jnp.stack([units[0][1], units[1][1]]),
            jnp.stack([units[0][0].reshape(512), units[1][0].reshape(512)]).reshape(1, 1024),
        ]
    )
    early = jnp.concatenate([early, unit_rows], axis=0)
    early = jnp.sum(share(early, PLANE_CORES, 32), axis=0)
    late = jnp.stack([shared[0][1], shared[0][2]])
    late = jnp.sum(share(late, "z", 4), axis=0)
    late = jnp.sum(share(late, PLANE_CORES, 32), axis=0)

    sum_bout = jnp.stack([early[6], early[0]])
    sum_g1 = jnp.stack([late[0], early[1]])
    sum_s1 = jnp.stack([late[1], early[2]])
    sum_bdown = jnp.stack([early[7], early[3]])
    sum_g2 = jnp.stack([early[8], early[4]])
    sum_s2 = jnp.stack([early[9], early[5]])
    sum_bup = lax.dynamic_index_in_dim(early[10:12].reshape(2, 2, 512), lane, 1, False)
    sum_bqv = lax.dynamic_index_in_dim(early[12].reshape(2, 2, 2, CHUNK), lane, 2, False)

    grad_w_qkv = jnp.stack([attn_out[at][:, :384].reshape(64, 3, CHUNK) for at in range(layer_count)])
    grad_w_out = jnp.stack([attn_out[at][:, 384:].T for at in range(layer_count)])
    grad_w_up = jnp.stack([feed_out[at][:, :512] for at in range(layer_count)])
    grad_w_down = jnp.stack([feed_out[at][:, 512:].T for at in range(layer_count)])
    return (
        hidden_out,
        hidden_grad,
        grad_w_qkv,
        sum_bqv,
        grad_w_out,
        sum_bout,
        sum_g1,
        sum_s1,
        grad_w_up,
        sum_bup,
        grad_w_down,
        sum_bdown,
        sum_g2,
        sum_s2,
    )


def solution(mesh):
    inner = Mesh(mesh.devices.reshape(2, 4, 2, 4, 2), AXES)
    dp = ("xh", "y", "c")
    tensor = ("z", "xl")
    rows = dp + tensor
    in_specs = (
        P(rows, None),
        P(rows),
        P(None, dp, None, tensor),
        P(None, None, tensor),
        P(None, tensor, dp),
        P(),
        P(),
        P(),
        P(None, dp, tensor),
        P(None, tensor),
        P(None, tensor, dp),
        P(),
        P(),
        P(),
        P(rows, None),
    )
    out_specs = (
        P(rows, None),
        P(rows, None),
        P(None, dp, None, tensor),
        P(None, None, tensor),
        P(None, tensor, dp),
        P(),
        P(),
        P(),
        P(None, dp, tensor),
        P(None, tensor),
        P(None, tensor, dp),
        P(),
        P(),
        P(),
    )
    return jax.shard_map(local, mesh=inner, in_specs=in_specs, out_specs=out_specs, check_vma=False)
```

```python
import functools

import jax
import jax.numpy as jnp
from jax import lax
from jax.experimental import pallas as pl
from jax.experimental.pallas import tpu as pltpu
from jax.sharding import Mesh
from jax.sharding import PartitionSpec as P

HEAD_DIM = 64
eps = 1e-05
big_negative = -1e30
score_scale = HEAD_DIM ** (-0.5)

AXES = ("xh", "y", "c", "z", "xl")
PLANE = ("xl", "xh", "y")
PLANE_CORES = ("xl", "xh", "y", "c")
CHUNK = 128
WIDTH = 1024
HALF = 512
GROUP_ROWS = 512
MIB = 1024 * 1024
BDOWN, BOUT, G1, S1, G2, S2 = range(6)


def swap_rows(values):
    return lax.ppermute(values, ("c", "xl"), [(0, 0), (1, 2), (2, 1), (3, 3)])


def other_core(values):
    return lax.ppermute(values, "c", [(0, 1), (1, 0)])


def share(values, axis, count):
    copies = jnp.broadcast_to(values[None], (count,) + values.shape)
    return lax.all_to_all(copies, axis, 0, 0, tiled=True)


def from_ahead(values, step):
    return lax.ppermute(values, "z", [((at + step) % 4, at) for at in range(4)])


def to_ahead(values, step):
    return lax.ppermute(values, "z", [(at, (at + step) % 4) for at in range(4)])


def gather_z(rows):
    return [rows] + [from_ahead(rows, step) for step in AHEAD[1:]]


AHEAD = (0, 2, 1, 3)


def tie(first, second):
    return lax.optimization_barrier((first, second))


def scatter_z(parts):
    return [parts[0]] + [to_ahead(part, step) for part, step in zip(parts[1:], AHEAD[1:])]


def last_block(at, rank, step):
    return (0,) * (rank - 1) + (at,)


def call(kernel, ins, outs, scratch=(), vmem=32, flops=1_200_000_000, after=()):
    specs, arrays, size = [], [], 0
    for one in ins[1:]:
        if isinstance(one, tuple):
            one, cols, at = one
            shape = one.shape[:-1] + (cols,)
            place_of = functools.partial(last_block, at, len(shape))
            specs.append(pl.BlockSpec(shape, place_of, pipeline_mode=pl.Buffered(1)))
        else:
            shape = one.shape
            specs.append(pl.BlockSpec(memory_space=pltpu.VMEM))
        arrays.append(one)
        count = 1
        for extent in shape:
            count *= extent
        size += count * one.dtype.itemsize
    size += sum(one.size * one.dtype.itemsize for one in outs)
    count = len(arrays)

    def body(place, *refs):
        kernel(place, *refs[:count], *refs[count + len(after) :])

    return pl.pallas_call(
        body,
        out_shape=tuple(outs),
        grid=(1,) if any(isinstance(one, tuple) for one in ins) else (),
        in_specs=[pl.BlockSpec(memory_space=pltpu.SMEM)]
        + specs
        + [pl.BlockSpec(memory_space=pl.ANY)] * len(after),
        out_specs=tuple([pl.BlockSpec(memory_space=pltpu.VMEM)] * len(outs)),
        scratch_shapes=list(scratch),
        compiler_params=pltpu.CompilerParams(vmem_limit_bytes=vmem * MIB),
        cost_estimate=pl.CostEstimate(flops=flops, bytes_accessed=size, transcendentals=0),
        name=kernel.__name__,
    )(ins[0], *arrays, *after)


def bf(*shape):
    return jax.ShapeDtypeStruct(shape, jnp.bfloat16)


def fl(*shape):
    return jax.ShapeDtypeStruct(shape, jnp.float32)


def nt_dot(left, right):
    return lax.dot_general(left, right, (((1,), (1,)), ((), ())), preferred_element_type=jnp.float32)


def nn_dot(left, right):
    return jnp.dot(left, right, preferred_element_type=jnp.float32)


def own_order(values, core):
    even = [values[:, at : at + 64] for at in range(0, WIDTH, 128)]
    odd = [values[:, at + 64 : at + 128] for at in range(0, WIDTH, 128)]
    even, odd = jnp.concatenate(even, axis=1), jnp.concatenate(odd, axis=1)
    mine = jnp.where(core == 0, even, odd)
    theirs = jnp.where(core == 0, odd, even)
    return jnp.concatenate([mine, theirs], axis=1)


def natural_order(values, core):
    mine, theirs = values[:, :HALF], values[:, HALF:]
    even = jnp.where(core == 0, mine, theirs)
    odd = jnp.where(core == 0, theirs, mine)
    pieces = []
    for at in range(0, HALF, 64):
        pieces += [even[:, at : at + 64], odd[:, at : at + 64]]
    return jnp.concatenate(pieces, axis=1)


def normalize(values):
    center = values - jnp.mean(values, axis=-1, keepdims=True)
    spread = jnp.mean(center * center, axis=-1, keepdims=True)
    factor = lax.rsqrt(spread + eps)
    return center * factor, factor


def row(ref, at):
    return ref[at : at + 1, :]


def total(refs, rows=slice(None)):
    result = refs[0][rows, :].astype(jnp.float32)
    for one in refs[1:]:
        result = result + one[rows, :].astype(jnp.float32)
    return result


def enter_grad(place, gout_ref, low_ref, gsum_ref):
    grad = gout_ref[...].astype(jnp.float32)
    gsum_ref[...] = jnp.broadcast_to(jnp.sum(grad, axis=0, keepdims=True), (8, WIDTH))
    low_ref[...] = own_order(grad, place[0]).astype(jnp.bfloat16)


def enter(place, x_ref, vec_ref, resid_ref, low_ref, vecs_ref):
    core = place[0]
    vecs = own_order(vec_ref[...], core)
    vecs_ref[...] = vecs
    resid = own_order(x_ref[:CHUNK, :].astype(jnp.float32), core)
    resid_ref[...] = resid
    scaled, _ = normalize(resid)
    low_ref[:CHUNK, :] = (scaled * vecs[G1 : G1 + 1] + vecs[S1 : S1 + 1]).astype(jnp.bfloat16)
    low_ref[CHUNK:, :] = x_ref[CHUNK:, :]


def add_and_norm(bias_at, gain_at, shift_at):
    def add_norm(place, x_ref, p0, p1, p2, p3, vec_ref, next_ref, low_ref):
        values = x_ref[...] + total((p0, p1, p2, p3)) + row(vec_ref, bias_at)
        next_ref[...] = values
        scaled, _ = normalize(values)
        low_ref[...] = (scaled * row(vec_ref, gain_at) + row(vec_ref, shift_at)).astype(jnp.bfloat16)

    return add_norm


def add_and_leave(bias_at):
    def add_leave(place, x_ref, p0, p1, p2, p3, vec_ref, out_ref):
        values = x_ref[...] + total((p0, p1, p2, p3)) + row(vec_ref, bias_at)
        out_ref[...] = natural_order(values, place[0]).astype(jnp.bfloat16)

    return add_leave


def norm_back(gain_at, last, riders=False):
    def norm_backward(place, x_ref, g_ref, p0, p1, p2, p3, vec_ref, grad_ref, *more):
        core = place[0]
        if riders:
            more[-1][...] = rider_total((p0, p1, p2, p3))
            more = more[:-1]
        d_norm = total((p0, p1, p2, p3), slice(0, CHUNK))
        scaled, factor = normalize(x_ref[...])
        inner = d_norm * row(vec_ref, gain_at)
        mean_one = jnp.mean(inner, axis=-1, keepdims=True)
        mean_two = jnp.mean(inner * scaled, axis=-1, keepdims=True)
        grad = g_ref[...].astype(jnp.float32) + factor * (inner - mean_one - scaled * mean_two)
        low = grad.astype(jnp.bfloat16)
        sums = [
            jnp.sum(d_norm * scaled, axis=0, keepdims=True),
            jnp.sum(d_norm, axis=0, keepdims=True),
            jnp.sum(low.astype(jnp.float32), axis=0, keepdims=True),
            jnp.zeros((5, WIDTH), jnp.float32),
        ]
        if last:
            grad_ref[...] = natural_order(grad, core)
        else:
            grad_ref[...] = grad
            more[0][...] = low
        more[-1][...] = natural_order(jnp.concatenate(sums, axis=0), core)

    return norm_backward


def pack_norms(place, grad_ref, mid_ref, end_ref, out_ref):
    out_ref[0:1, :] = row(grad_ref, 0)
    out_ref[1:2, :] = row(mid_ref, 2)
    out_ref[2:4, :] = end_ref[0:2, :]
    out_ref[4:6, :] = mid_ref[0:2, :]
    out_ref[6:8, :] = jnp.zeros((2, WIDTH), jnp.float32)


def pack_middle(place, before_ref, mid_ref, out_ref):
    out_ref[0:1, :] = row(before_ref, 2)
    out_ref[1:2, :] = row(mid_ref, 2)
    out_ref[2:4, :] = mid_ref[0:2, :]
    out_ref[4:8, :] = jnp.zeros((4, WIDTH), jnp.float32)


def queries_and_values(ref):
    return jnp.concatenate(
        [ref[0:1, :128], ref[0:1, 384:512], ref[0:1, 256:384], ref[0:1, 640:768]], axis=1
    )


def pack_units(place, sum_ref, up_ref, qkv_ref, out_ref):
    out_ref[...] = sum_ref[...]
    out_ref[6:7, :] = up_ref[0:1, :]
    out_ref[7:8, :HALF] = queries_and_values(qkv_ref)


def pack_riders(place, mid_ref, z0, z1, z2, z3, up_ref, qkv_ref, out_ref):
    late = total((z0, z1, z2, z3))
    rows = [mid_ref[at : at + 1, :] for at in range(4)] + [late[0:1], late[1:2], up_ref[0:1, :]]
    for at, one in enumerate(rows):
        out_ref[2 * at : 2 * at + 1, :] = one[:, :HALF]
        out_ref[2 * at + 1 : 2 * at + 2, :] = one[:, HALF:]
    out_ref[14:15, :] = queries_and_values(qkv_ref)
    out_ref[15:16, :] = jnp.zeros((1, HALF), jnp.float32)


def finish_sums(
    place, early_ref, rider_ref, bout_ref, g1_ref, s1_ref, bdown_ref, g2_ref, s2_ref, bup_ref, bqv_ref
):
    early = early_ref[:8, :] + early_ref[8:, :]
    riders = rider_ref[:16, :] + rider_ref[16:, :]

    def line(at):
        return jnp.concatenate([riders[2 * at : 2 * at + 1], riders[2 * at + 1 : 2 * at + 2]], axis=1)

    def put(ref, first, second):
        ref[0:1, :] = first
        ref[1:2, :] = second

    put(bdown_ref, line(0), early[0:1])
    put(bout_ref, line(1), early[1:2])
    put(g1_ref, line(4), early[2:3])
    put(s1_ref, line(5), early[3:4])
    put(g2_ref, line(2), early[4:5])
    put(s2_ref, line(3), early[5:6])
    first = place[2] == 0
    put(
        bup_ref,
        jnp.where(first, riders[12:13], riders[13:14]),
        jnp.where(first, early[6:7, :HALF], early[6:7, HALF:]),
    )
    for at, sums in enumerate((riders[14:15], early[7:8, :HALF])):
        for kind in range(2):
            pick = jnp.where(
                first,
                sums[:, kind * 256 : kind * 256 + CHUNK],
                sums[:, kind * 256 + CHUNK : kind * 256 + 256],
            )
            bqv_ref[2 * at + kind : 2 * at + kind + 1, :] = pick


def chunk_rows(place, step):
    at = lax.rem(place[1] + step, 4)
    return pl.ds(pl.multiple_of(at * CHUNK, CHUNK), CHUNK)


def assemble(place, pieces, full_ref):
    for piece, step in zip(pieces, AHEAD):
        full_ref[chunk_rows(place, step), :] = piece[...]


def hand_out(place, part_ref, outs):
    for out, step in zip(outs, AHEAD):
        out[:CHUNK, :] = part_ref[chunk_rows(place, step), :]


def ride_along(rider_ref, outs):
    high = rider_ref[...].astype(jnp.bfloat16)
    rest = rider_ref[...] - high.astype(jnp.float32)
    both = jnp.concatenate([high.astype(jnp.float32), rest], axis=0).astype(jnp.bfloat16)
    for out in outs:
        out[CHUNK:, :] = both


def rider_total(refs):
    both = total(refs, slice(CHUNK, CHUNK + 16))
    return both[:8] + both[8:]


def qkv_product(place, n0, n1, n2, n3, own_ref, other_ref, bias_ref, full_ref, qkv_ref, kv_ref):
    for piece, step in zip((n0, n1, n2, n3), AHEAD):
        full_ref[chunk_rows(place, step), :] = piece[:CHUNK, :]
    for block in range(2):
        cols = slice(block * 384, block * 384 + 384)
        out = nn_dot(full_ref[:, :HALF], own_ref[block, :, :384])
        out += nn_dot(full_ref[:, HALF:], other_ref[block, :, :384])
        low = (out + bias_ref[0:1, cols]).astype(jnp.bfloat16)
        qkv_ref[:, cols] = low
        kv_ref[:GROUP_ROWS, block * 256 : block * 256 + 256] = low[:, CHUNK:]


def qkv_product_first(
    place, n0, n1, n2, n3, own_ref, other_ref, bias_ref, full_ref, qkv_ref, kv_ref, seg_ref
):
    qkv_product(place, n0, n1, n2, n3, own_ref, other_ref, bias_ref, full_ref, qkv_ref, kv_ref)
    lines = [piece[CHUNK:, :CHUNK] for piece in (n0, n1, n2, n3)]
    for slot in range(4):
        line = lines[0]
        for piece, step in zip(lines[1:], AHEAD[1:]):
            line = jnp.where(lax.rem(place[1] + step, 4) == slot, piece, line)
        line = jnp.where(place[1] == slot, lines[0], line)
        seg_ref[:, slot * CHUNK : (slot + 1) * CHUNK] = line
        kv_ref[GROUP_ROWS:, slot * CHUNK : (slot + 1) * CHUNK] = line


def out_block(ref):
    return jnp.concatenate([ref[0, :, 384:512], ref[1, :, 384:512]], axis=1)


def feed_forward(
    place, n0, n1, n2, n3, own_ref, other_ref, bias_ref, full_ref, pre_ref, act_ref, o0, o1, o2, o3, part_ref
):
    assemble(place, (n0, n1, n2, n3), full_ref)
    for block in range(2):
        cols = slice(block * HALF, (block + 1) * HALF)
        pre = nn_dot(full_ref[:, :HALF], own_ref[block, :, :HALF])
        pre += nn_dot(full_ref[:, HALF:], other_ref[block, :, :HALF])
        pre += bias_ref[0:1, cols]
        pre_ref[:, cols] = pre
        act_ref[:, cols] = jax.nn.gelu(pre, approximate=True).astype(jnp.bfloat16)
    for half, ref in enumerate((own_ref, other_ref)):
        part = nt_dot(act_ref[:, :HALF], ref[0, :, HALF:]) + nt_dot(act_ref[:, HALF:], ref[1, :, HALF:])
        part_ref[:, half * HALF : (half + 1) * HALF] = part.astype(jnp.bfloat16)
    hand_out(place, part_ref, (o0, o1, o2, o3))


def gelu_slope(values):
    scale = 0.7978845608028654
    inner = scale * (values + 0.044715 * values * values * values)
    bend = jnp.tanh(inner)
    return 0.5 * (1.0 + bend) + 0.5 * values * (1.0 - bend * bend) * (
        scale * (1.0 + 3.0 * 0.044715 * values * values)
    )


def feed_backward(
    place, n0, n1, n2, n3, own_ref, other_ref, pre_ref, full_ref, dpre_ref, sum_ref, o0, o1, o2, o3, part_ref
):
    assemble(place, (n0, n1, n2, n3), full_ref)
    for block in range(2):
        cols = slice(block * HALF, (block + 1) * HALF)
        d_act = nn_dot(full_ref[:, :HALF], own_ref[block, :, HALF:])
        d_act += nn_dot(full_ref[:, HALF:], other_ref[block, :, HALF:])
        d_pre = (d_act * gelu_slope(pre_ref[:, cols])).astype(jnp.bfloat16)
        dpre_ref[:, cols] = d_pre
        sum_ref[0:1, cols] = jnp.sum(d_pre.astype(jnp.float32), axis=0, keepdims=True)
    for half, ref in enumerate((own_ref, other_ref)):
        part = nt_dot(dpre_ref[:, :HALF], ref[0, :, :HALF]) + nt_dot(dpre_ref[:, HALF:], ref[1, :, :HALF])
        part_ref[:, half * HALF : (half + 1) * HALF] = part.astype(jnp.bfloat16)
    hand_out(place, part_ref, (o0, o1, o2, o3))


def feed_backward_riders(place, rider_ref, *refs):
    feed_backward(place, *refs)
    ride_along(rider_ref, refs[-5:-1])


def qkv_backward_riders(place, rider_ref, *refs):
    qkv_backward(place, *refs)
    ride_along(rider_ref, refs[-5:-1])


def feed_weight_grads(place, norm_ref, dpre_ref, grad_ref, act_ref, keep_ref, give_ref, done_ref):
    done_ref[...] = jnp.zeros_like(done_ref)
    for first, left, right in ((0, norm_ref, dpre_ref), (HALF, grad_ref, act_ref)):
        for half, out in enumerate((keep_ref, give_ref)):
            left_t = left[:, half * HALF : (half + 1) * HALF].T
            for block in range(2):
                product = nn_dot(left_t, right[:, block * HALF : (block + 1) * HALF])
                out[block, :, first : first + HALF] = product.astype(jnp.bfloat16)


def attn_weight_grads(place, norm_ref, dqkv_ref, grad_ref, mixed_ref, keep_ref, give_ref, done_ref):
    done_ref[...] = jnp.zeros_like(done_ref)
    for half, out in enumerate((keep_ref, give_ref)):
        rows = slice(half * HALF, (half + 1) * HALF)
        norm_t = norm_ref[:, rows].T
        grad_t = grad_ref[:, rows].T
        outer = nn_dot(grad_t, mixed_ref[...]).astype(jnp.bfloat16)
        for block in range(2):
            product = nn_dot(norm_t, dqkv_ref[:, block * 384 : block * 384 + 384])
            out[block, :, :384] = product.astype(jnp.bfloat16)
            out[block, :, 384:] = outer[:, block * CHUNK : (block + 1) * CHUNK]


def mix_gradient(place, n0, n1, n2, n3, own_ref, other_ref, full_ref, dmix_ref):
    assemble(place, (n0, n1, n2, n3), full_ref)
    d_mix = nn_dot(full_ref[:, :HALF], out_block(own_ref)) + nn_dot(
        full_ref[:, HALF:], out_block(other_ref)
    )
    dmix_ref[...] = d_mix.astype(jnp.bfloat16)


def qkv_backward(
    place, dq_ref, mine_ref, came_ref, own_ref, other_ref, dqkv_ref, sum_ref, o0, o1, o2, o3, part_ref
):
    d_kv = (mine_ref[...] + came_ref[...].astype(jnp.float32)).astype(jnp.bfloat16)
    for block in range(2):
        base = block * 384
        dqkv_ref[:, base : base + CHUNK] = dq_ref[:, block * CHUNK : (block + 1) * CHUNK]
        dqkv_ref[:, base + CHUNK : base + 384] = d_kv[:, block * 256 : block * 256 + 256]
    sum_ref[0:1, :] = jnp.sum(dqkv_ref[...].astype(jnp.float32), axis=0, keepdims=True)
    for half, ref in enumerate((own_ref, other_ref)):
        part = nt_dot(dqkv_ref[:, :384], ref[0, :, :384]) + nt_dot(dqkv_ref[:, 384:], ref[1, :, :384])
        part_ref[:, half * HALF : (half + 1) * HALF] = part.astype(jnp.bfloat16)
    hand_out(place, part_ref, (o0, o1, o2, o3))


def interleave(own, other):
    pieces = []
    for at in range(own.shape[0] // CHUNK):
        pieces += [own[at * CHUNK : (at + 1) * CHUNK], other[at * CHUNK : (at + 1) * CHUNK]]
    return jnp.concatenate(pieces, axis=0)


def by_head(block):
    first = lax.broadcasted_iota(jnp.int32, block.shape, 1) < HEAD_DIM
    zero = jnp.zeros_like(block)
    return jnp.concatenate([jnp.where(first, block, zero), jnp.where(first, zero, block)], axis=0)


def pick_heads(both):
    first = lax.broadcasted_iota(jnp.int32, (CHUNK, CHUNK), 0) < HEAD_DIM
    return jnp.where(first, both[:, :CHUNK], both[:, CHUNK:]).T


def tile_masks(place, own_ref, other_ref):
    down = lax.broadcasted_iota(jnp.int32, (CHUNK, CHUNK), 0)
    across = lax.broadcasted_iota(jnp.int32, (CHUNK, CHUNK), 1)
    tiles = GROUP_ROWS // CHUNK

    def line(ref, at):
        return ref[0:1, at * CHUNK : (at + 1) * CHUNK].astype(jnp.float32)

    def column(ref, at):
        return jnp.broadcast_to(line(ref, at), (CHUNK, CHUNK)).T

    own = [column(own_ref, at) for at in range(tiles)]
    other = [column(other_ref, at) for at in range(tiles)]
    masks = []
    for at in range(tiles):
        rows = line(own_ref, at)
        used = rows >= 0.0
        blocks = []
        for key_at in range(at + 1):
            from_own = (own[key_at] == rows) & used
            from_other = (other[key_at] == rows) & used
            if key_at == at:
                from_own = (from_own & (down <= across)) | (down == across)
                from_other = from_other & (place[0] == 1)
            blocks += [jnp.where(from_own, 0.0, big_negative), jnp.where(from_other, 0.0, big_negative)]
        mask = jnp.concatenate(blocks, axis=0)
        masks.append(jnp.concatenate([mask, mask], axis=1))
    return masks


def masked_scores(keys_all, q_heads, bias):
    scores = nt_dot(keys_all, q_heads) * score_scale
    return jnp.where(bias < 0.0, big_negative, scores)


def kv_blocks(qkv_ref, kv_ref, block):
    base = block * 3 * CHUNK
    k_own = qkv_ref[:, base + CHUNK : base + 2 * CHUNK]
    v_own = qkv_ref[:, base + 2 * CHUNK : base + 3 * CHUNK]
    k_other = kv_ref[:GROUP_ROWS, block * 2 * CHUNK : block * 2 * CHUNK + CHUNK]
    v_other = kv_ref[:GROUP_ROWS, block * 2 * CHUNK + CHUNK : block * 2 * CHUNK + 2 * CHUNK]
    return interleave(k_own, k_other), interleave(v_own, v_other)


def attend_forward(
    place, qkv_ref, kv_ref, seg_ref, seg_other_ref, own_ref, other_ref, mixed_ref, lse_ref, o0, o1, o2, o3, part_ref
):
    tiles = GROUP_ROWS // CHUNK
    biases = tile_masks(place, seg_ref, seg_other_ref)
    for block in range(2):
        base = block * 3 * CHUNK
        keys_all, values_all = kv_blocks(qkv_ref, kv_ref, block)
        values_t = values_all.T
        for at in range(tiles):
            rows = slice(at * CHUNK, (at + 1) * CHUNK)
            count = 2 * CHUNK * (at + 1)
            q_heads = by_head(qkv_ref[rows, base : base + CHUNK])
            scores = masked_scores(keys_all[:count], q_heads, biases[at])
            top = jnp.max(scores, axis=0, keepdims=True)
            expo = jnp.exp(scores - top)
            weight = jnp.sum(expo, axis=0, keepdims=True)
            prob = (expo * (1.0 / weight)).astype(jnp.bfloat16)
            mixed = pick_heads(nn_dot(values_t[:, :count], prob))
            mixed_ref[rows, block * CHUNK : (block + 1) * CHUNK] = mixed.astype(jnp.bfloat16)
            lse = top + jnp.log(weight)
            lse_ref[2 * block : 2 * block + 1, rows] = lse[:, :CHUNK]
            lse_ref[2 * block + 1 : 2 * block + 2, rows] = lse[:, CHUNK:]
    for half, ref in enumerate((own_ref, other_ref)):
        part = nt_dot(mixed_ref[...], out_block(ref))
        part_ref[:, half * HALF : (half + 1) * HALF] = part.astype(jnp.bfloat16)
    hand_out(place, part_ref, (o0, o1, o2, o3))


def attend_backward(
    place, qkv_ref, kv_ref, seg_ref, seg_other_ref, lse_ref, dmix_ref, dq_ref, own_ref, other_ref, dk_ref, dv_ref
):
    tiles = GROUP_ROWS // CHUNK
    biases = tile_masks(place, seg_ref, seg_other_ref)
    for block in range(2):
        base = block * 3 * CHUNK
        keys_all, values_all = kv_blocks(qkv_ref, kv_ref, block)
        keys_t = keys_all.T
        for at in reversed(range(tiles)):
            rows = slice(at * CHUNK, (at + 1) * CHUNK)
            count = 2 * CHUNK * (at + 1)
            q_heads = by_head(qkv_ref[rows, base : base + CHUNK])
            dm_heads = by_head(dmix_ref[rows, block * CHUNK : (block + 1) * CHUNK])
            lse = jnp.concatenate(
                [lse_ref[2 * block : 2 * block + 1, rows], lse_ref[2 * block + 1 : 2 * block + 2, rows]],
                axis=1,
            )
            scores = masked_scores(keys_all[:count], q_heads, biases[at])
            prob = jnp.exp(scores - lse)
            dprob = nt_dot(values_all[:count], dm_heads)
            weighted = jnp.sum(prob * dprob, axis=0, keepdims=True)
            dscore = (prob * (dprob - weighted)).astype(jnp.bfloat16)
            prob_low = prob.astype(jnp.bfloat16)
            dq = pick_heads(nn_dot(keys_t[:, :count], dscore)) * score_scale
            dq_ref[rows, block * CHUNK : (block + 1) * CHUNK] = dq.astype(jnp.bfloat16)
            dk = nn_dot(dscore, q_heads) * score_scale
            dv = nn_dot(prob_low, dm_heads)
            if at == tiles - 1:
                dk_ref[...] = dk
                dv_ref[...] = dv
            else:
                dk_ref[:count] += dk
                dv_ref[:count] += dv
        for at in range(tiles):
            rows = slice(at * CHUNK, (at + 1) * CHUNK)
            mine = slice(2 * at * CHUNK, (2 * at + 1) * CHUNK)
            theirs = slice((2 * at + 1) * CHUNK, (2 * at + 2) * CHUNK)
            k_cols = slice(block * 2 * CHUNK, block * 2 * CHUNK + CHUNK)
            v_cols = slice(block * 2 * CHUNK + CHUNK, block * 2 * CHUNK + 2 * CHUNK)
            own_ref[rows, k_cols] = dk_ref[mine]
            own_ref[rows, v_cols] = dv_ref[mine]
            other_ref[rows, k_cols] = dk_ref[theirs].astype(jnp.bfloat16)
            other_ref[rows, v_cols] = dv_ref[theirs].astype(jnp.bfloat16)


def local(
    hidden_in,
    segment_ids,
    w_qkv,
    b_qv,
    w_out,
    b_out,
    ln1_gain,
    ln1_bias,
    w_up,
    b_up,
    w_down,
    b_down,
    ln2_gain,
    ln2_bias,
    out_grad,
):
    layer_count = w_qkv.shape[0]
    core = lax.axis_index("c")
    lane = lax.axis_index("xl")
    place = jnp.stack([core, lax.axis_index("z"), lane]).astype(jnp.int32)

    ids = segment_ids.astype(jnp.bfloat16).reshape(1, CHUNK)
    ids = jnp.pad(ids, ((0, 15), (0, WIDTH - CHUNK)))
    moved = swap_rows(jnp.concatenate([hidden_in, ids], axis=0))
    moved_grad = swap_rows(out_grad)
    vec_rows = []
    for at in range(layer_count):
        vec_rows += [b_down[at], b_out[at], ln1_gain[at], ln1_bias[at], ln2_gain[at], ln2_bias[at]]
    vecs = jnp.concatenate([jnp.stack(vec_rows), jnp.zeros((4, WIDTH), jnp.float32)], axis=0)

    attn_slab = [
        jnp.concatenate([w_qkv[at].reshape(64, 3 * CHUNK), w_out[at].T], axis=1)
        for at in range(layer_count)
    ]
    feed_slab = [jnp.concatenate([w_up[at], w_down[at].T], axis=1) for at in range(layer_count)]
    attn_own = [share(attn_slab[0], PLANE, 16).reshape(2, HALF, 512)]

    resid, normed, vecs = call(
        enter,
        [place, moved, vecs],
        [fl(CHUNK, WIDTH), bf(CHUNK + 16, WIDTH), fl(16, WIDTH)],
        vmem=6,
    )
    bias_mine = jnp.concatenate([b_qv.reshape(layer_count, 2 * CHUNK), b_up], axis=1)
    bias_next = lax.ppermute(bias_mine, "xl", [(0, 1), (1, 0)])
    bias_both = jnp.stack(
        [jnp.where(lane == 0, bias_mine, bias_next), jnp.where(lane == 0, bias_next, bias_mine)], axis=1
    )

    pieces = gather_z(normed)
    pieces, (bias_both, moved_grad) = tie(pieces, (bias_both, moved_grad))
    attn_w = [(attn_own[0], other_core(attn_own[0]))]
    feed_w = []
    attn_own.append(share(attn_slab[1], PLANE, 16).reshape(2, HALF, 512))
    feed_own = [None, share(feed_slab[1], PLANE, 16).reshape(2, HALF, 1024)]
    grad, grad_sum = call(enter_grad, [place, moved_grad], [bf(CHUNK, WIDTH), fl(8, WIDTH)], vmem=6)
    lows = gather_z(grad)

    part_scratch = [pltpu.VMEM((GROUP_ROWS, WIDTH), jnp.bfloat16)]
    full = bf(GROUP_ROWS, WIDTH)
    piece = bf(CHUNK, WIDTH)

    saved = []
    for at in range(layer_count):
        base = 6 * at
        zero = jnp.zeros((2, CHUNK), jnp.float32)
        qkv_bias = jnp.concatenate(
            [bias_both[at][:, :CHUNK], zero, bias_both[at][:, CHUNK : 2 * CHUNK]], axis=1
        ).reshape(1, 6 * CHUNK)
        up_bias = bias_both[at][:, 2 * CHUNK :].reshape(1, 1024)
        first = at == 0
        normed_full, qkv, kv_mine, *ids = call(
            qkv_product_first if first else qkv_product,
            [place, *pieces, *attn_w[at], qkv_bias],
            [full, bf(GROUP_ROWS, 768), bf(GROUP_ROWS + 16 * first, 512)] + [bf(16, 512)] * first,
            flops=2200000000,
            vmem=11,
            after=[grad] if first else (),
        )
        kv_other = other_core(kv_mine)
        if first:
            segs, segs_other = ids[0], kv_other[GROUP_ROWS:]
            feed_slab[0], (segs, lows) = tie(feed_slab[0], (segs, lows))
            feed_own[0] = share(feed_slab[0], PLANE, 16).reshape(2, HALF, 1024)
        mixed, lse, *parts = call(
            attend_forward,
            [place, qkv, kv_other, segs, segs_other, *attn_w[at]],
            [bf(GROUP_ROWS, 256), fl(8, GROUP_ROWS), piece, piece, piece, piece],
            part_scratch,
            flops=6300000000,
            vmem=16,
            after=() if first else [feed_own[1]],
        )
        resid_mid, cnorm = call(
            add_and_norm(base + BOUT, base + G2, base + S2),
            [place, resid, *scatter_z(parts), vecs],
            [fl(CHUNK, WIDTH), piece],
            vmem=6,
        )
        cnorm, feed_own[at] = tie(cnorm, feed_own[at])
        feed_w.append((feed_own[at], other_core(feed_own[at])))
        cnorm_full, pre_up, act, *parts = call(
            feed_forward,
            [place, *gather_z(cnorm), *feed_w[at], up_bias],
            [full, fl(GROUP_ROWS, WIDTH), full, piece, piece, piece, piece],
            part_scratch,
            flops=5200000000,
            vmem=18,
        )
        saved.append((resid, normed_full, qkv, kv_other, mixed, lse, resid_mid, cnorm_full, pre_up, act))
        parts = scatter_z(parts)
        if at < layer_count - 1:
            resid, normed = call(
                add_and_norm(base + BDOWN, base + 6 + G1, base + 6 + S1),
                [place, resid_mid, *parts, vecs],
                [fl(CHUNK, WIDTH), piece],
                vmem=6,
            )
            normed, attn_own[1] = tie(normed, attn_own[1])
            attn_w.append((attn_own[1], other_core(attn_own[1])))
            pieces = gather_z(normed)
    last_parts = parts

    attn_out = [None] * layer_count
    feed_out = [None] * layer_count
    for at in reversed(range(layer_count)):
        base = 6 * at
        resid_in, normed_full, qkv, kv_other, mixed, lse, resid_mid, cnorm_full, pre_up, act = saved[at]

        top = at == layer_count - 1
        sent = piece if top else bf(CHUNK + 16, WIDTH)
        low_full, d_pre, bup_sum, *parts = call(
            feed_backward if top else feed_backward_riders,
            [place, *(() if top else (early,)), *lows, *feed_w[at], pre_up],
            [full, full, fl(1, WIDTH), sent, sent, sent, sent],
            part_scratch,
            flops=5800000000,
            vmem=18,
            after=() if top else [feed_came],
        )
        arrived = scatter_z(parts)
        keep, give, done = call(
            feed_weight_grads,
            [place, cnorm_full, d_pre, low_full, act],
            [bf(2, HALF, 1024), bf(2, HALF, 1024), fl(8, CHUNK)],
            flops=3500000000,
            vmem=18,
            after=last_parts[1:] if top else (),
        )
        feed_sum = (keep.astype(jnp.float32) + other_core(give).astype(jnp.float32)).astype(jnp.bfloat16)
        arrived, done = tie(arrived, done)
        grad, low, mid_sums, *early_sum = call(
            norm_back(base + G2, False, not top),
            [place, resid_mid, grad, *arrived, vecs],
            [fl(CHUNK, WIDTH), piece, fl(8, WIDTH)] + [fl(8, WIDTH)] * (not top),
            vmem=6,
            after=[done] if top else [done, attn_came],
        )

        middle = gather_z(low)
        if at == 0:
            (riders,) = call(pack_middle, [place, sums, mid_sums], [fl(8, WIDTH)], vmem=4)
            (early,) = call(
                pack_units, [place, early_sum[0], *before], [fl(8, WIDTH)], vmem=4
            )
            early = early + other_core(early)
            high = early.astype(jnp.bfloat16)
            rest = (early - high.astype(jnp.float32)).astype(jnp.bfloat16)
            early = jnp.broadcast_to(jnp.concatenate([high, rest])[None], (16, 16, WIDTH))
            payload = jnp.concatenate([feed_sum.reshape(16, 64, 1024), early], axis=1)
            feed_came = lax.all_to_all(payload, PLANE, 0, 0, tiled=True)
            came = jnp.sum(feed_came.astype(jnp.float32), axis=0)
            feed_out[0], early = came[:64], came[64:]
        else:
            feed_came = lax.all_to_all(feed_sum.reshape(16, 64, 1024), PLANE, 0, 0, tiled=True)
            feed_out[at] = jnp.sum(feed_came.astype(jnp.float32), axis=0)
        low_full, d_mix = call(
            mix_gradient,
            [place, *middle, *attn_w[at]],
            [full, bf(GROUP_ROWS, 256)],
            flops=1200000000,
            vmem=8,
            after=[feed_sum],
        )
        d_q, d_own, d_other = call(
            attend_backward,
            [place, qkv, kv_other, segs, segs_other, lse, d_mix],
            [bf(GROUP_ROWS, 256), fl(GROUP_ROWS, 512), bf(GROUP_ROWS, 512)],
            [pltpu.VMEM((2 * GROUP_ROWS, CHUNK), jnp.float32)] * 2,
            flops=7700000000,
            vmem=16,
        )
        d_qkv, bqkv_sum, *parts = call(
            qkv_backward if top else qkv_backward_riders,
            [place, *(() if top else (riders,)), d_q, d_own, other_core(d_other), *attn_w[at]],
            [bf(GROUP_ROWS, 768), fl(1, 768), sent, sent, sent, sent],
            part_scratch,
            flops=2300000000,
            vmem=11,
        )
        if top:
            (hidden,) = call(
                add_and_leave(base + BDOWN), [place, resid_mid, *last_parts, vecs], [piece], vmem=6
            )
            hidden_out = swap_rows(hidden)
        arrived = scatter_z(parts)
        keep, give, done = call(
            attn_weight_grads,
            [place, normed_full, d_qkv, low_full, mixed],
            [bf(2, HALF, 512), bf(2, HALF, 512), fl(8, CHUNK)],
            flops=2600000000,
            vmem=11,
        )
        attn_sum = (keep.astype(jnp.float32) + other_core(give).astype(jnp.float32)).astype(jnp.bfloat16)
        arrived, done = tie(arrived, done)
        more = [piece, fl(8, WIDTH)] if top else [fl(8, WIDTH), fl(8, WIDTH)]
        grad, *rest = call(
            norm_back(base + G1, at == 0, not top),
            [place, resid_in, grad, *arrived, vecs],
            [fl(CHUNK, WIDTH), *more],
            vmem=6,
            after=[hidden_out, done] if top else [hidden_out, done, feed_came],
        )

        if at > 0:
            low, sums = rest
            attn_came = lax.all_to_all(attn_sum.reshape(16, 64, 512), PLANE, 0, 0, tiled=True)
            attn_out[at] = jnp.sum(attn_came.astype(jnp.float32), axis=0)
            lows = gather_z(low)
            (early,) = call(pack_norms, [place, grad_sum, mid_sums, sums], [fl(8, WIDTH)], vmem=4)
            before = [bup_sum, bqkv_sum]
        else:
            sums, riders = rest
            late = gather_z(sums)
            (riders,) = call(
                pack_riders, [place, riders, *late, bup_sum, bqkv_sum], [fl(16, HALF)], vmem=4
            )
            riders = riders + other_core(riders)
            high = riders.astype(jnp.bfloat16)
            rest = (riders - high.astype(jnp.float32)).astype(jnp.bfloat16)
            riders = jnp.broadcast_to(jnp.concatenate([high, rest])[None], (16, 32, HALF))
            payload = jnp.concatenate([attn_sum.reshape(16, 64, 512), riders], axis=1)
            hidden_grad, payload = tie(swap_rows(grad), payload)
            came = lax.all_to_all(payload, PLANE, 0, 0, tiled=True)
            came = jnp.sum(came.astype(jnp.float32), axis=0)
            attn_out[at] = came[:64]

    sum_bout, sum_g1, sum_s1, sum_bdown, sum_g2, sum_s2, sum_bup, sum_bqv = call(
        finish_sums,
        [place, early, came[64:]],
        [fl(2, WIDTH)] * 6 + [fl(2, 512), fl(4, CHUNK)],
        vmem=6,
    )
    sum_bqv = sum_bqv.reshape(2, 2, CHUNK)

    grad_w_qkv = jnp.stack([attn_out[at][:, :384].reshape(64, 3, CHUNK) for at in range(layer_count)])
    grad_w_out = jnp.stack([attn_out[at][:, 384:].T for at in range(layer_count)])
    grad_w_up = jnp.stack([feed_out[at][:, :512] for at in range(layer_count)])
    grad_w_down = jnp.stack([feed_out[at][:, 512:].T for at in range(layer_count)])
    return (
        hidden_out,
        hidden_grad,
        grad_w_qkv,
        sum_bqv,
        grad_w_out,
        sum_bout,
        sum_g1,
        sum_s1,
        grad_w_up,
        sum_bup,
        grad_w_down,
        sum_bdown,
        sum_g2,
        sum_s2,
    )


def solution(mesh):
    inner = Mesh(mesh.devices.reshape(2, 4, 2, 4, 2), AXES)
    dp = ("xh", "y", "c")
    tensor = ("z", "xl")
    rows = dp + tensor
    in_specs = (
        P(rows, None),
        P(rows),
        P(None, dp, None, tensor),
        P(None, None, tensor),
        P(None, tensor, dp),
        P(),
        P(),
        P(),
        P(None, dp, tensor),
        P(None, tensor),
        P(None, tensor, dp),
        P(),
        P(),
        P(),
        P(rows, None),
    )
    out_specs = (
        P(rows, None),
        P(rows, None),
        P(None, dp, None, tensor),
        P(None, None, tensor),
        P(None, tensor, dp),
        P(),
        P(),
        P(),
        P(None, dp, tensor),
        P(None, tensor),
        P(None, tensor, dp),
        P(),
        P(),
        P(),
    )
    return jax.shard_map(local, mesh=inner, in_specs=in_specs, out_specs=out_specs, check_vma=False)
```

```python
import functools

import jax
import jax.numpy as jnp
from jax import lax
from jax.experimental import pallas as pl
from jax.experimental.pallas import tpu as pltpu
from jax.sharding import Mesh
from jax.sharding import PartitionSpec as P

HEAD_DIM = 64
eps = 1e-05
big_negative = -1e30
score_scale = HEAD_DIM ** (-0.5)

AXES = ("xh", "y", "c", "z", "xl")
PLANE = ("xl", "xh", "y")
PLANE_CORES = ("xl", "xh", "y", "c")
CHUNK = 128
WIDTH = 1024
HALF = 512
GROUP_ROWS = 512
MIB = 1024 * 1024
BDOWN, BOUT, G1, S1, G2, S2 = range(6)


def swap_rows(values):
    return lax.ppermute(values, ("c", "xl"), [(0, 0), (1, 2), (2, 1), (3, 3)])


def other_core(values):
    return lax.ppermute(values, "c", [(0, 1), (1, 0)])


def share(values, axis, count):
    copies = jnp.broadcast_to(values[None], (count,) + values.shape)
    return lax.all_to_all(copies, axis, 0, 0, tiled=True)


def from_ahead(values, step):
    return lax.ppermute(values, "z", [((at + step) % 4, at) for at in range(4)])


def to_ahead(values, step):
    return lax.ppermute(values, "z", [(at, (at + step) % 4) for at in range(4)])


def gather_z(rows):
    return [rows] + [from_ahead(rows, step) for step in AHEAD[1:]]


AHEAD = (0, 2, 1, 3)


def tie(first, second):
    return lax.optimization_barrier((first, second))


def scatter_z(parts):
    return [parts[0]] + [to_ahead(part, step) for part, step in zip(parts[1:], AHEAD[1:])]


def last_block(at, rank, step):
    return (0,) * (rank - 1) + (at,)


def call(kernel, ins, outs, scratch=(), vmem=32, flops=1_200_000_000, after=()):
    specs, arrays, size = [], [], 0
    for one in ins[1:]:
        if isinstance(one, tuple):
            one, cols, at = one
            shape = one.shape[:-1] + (cols,)
            place_of = functools.partial(last_block, at, len(shape))
            specs.append(pl.BlockSpec(shape, place_of, pipeline_mode=pl.Buffered(1)))
        else:
            shape = one.shape
            specs.append(pl.BlockSpec(memory_space=pltpu.VMEM))
        arrays.append(one)
        count = 1
        for extent in shape:
            count *= extent
        size += count * one.dtype.itemsize
    size += sum(one.size * one.dtype.itemsize for one in outs)
    count = len(arrays)

    def body(place, *refs):
        kernel(place, *refs[:count], *refs[count + len(after) :])

    return pl.pallas_call(
        body,
        out_shape=tuple(outs),
        grid=(1,) if any(isinstance(one, tuple) for one in ins) else (),
        in_specs=[pl.BlockSpec(memory_space=pltpu.SMEM)]
        + specs
        + [pl.BlockSpec(memory_space=pl.ANY)] * len(after),
        out_specs=tuple([pl.BlockSpec(memory_space=pltpu.VMEM)] * len(outs)),
        scratch_shapes=list(scratch),
        compiler_params=pltpu.CompilerParams(vmem_limit_bytes=vmem * MIB),
        cost_estimate=pl.CostEstimate(flops=flops, bytes_accessed=size, transcendentals=0),
        name=kernel.__name__,
    )(ins[0], *arrays, *after)


def bf(*shape):
    return jax.ShapeDtypeStruct(shape, jnp.bfloat16)


def fl(*shape):
    return jax.ShapeDtypeStruct(shape, jnp.float32)


def nt_dot(left, right):
    return lax.dot_general(left, right, (((1,), (1,)), ((), ())), preferred_element_type=jnp.float32)


def nn_dot(left, right):
    return jnp.dot(left, right, preferred_element_type=jnp.float32)


def own_order(values, core):
    even = [values[:, at : at + 64] for at in range(0, WIDTH, 128)]
    odd = [values[:, at + 64 : at + 128] for at in range(0, WIDTH, 128)]
    even, odd = jnp.concatenate(even, axis=1), jnp.concatenate(odd, axis=1)
    mine = jnp.where(core == 0, even, odd)
    theirs = jnp.where(core == 0, odd, even)
    return jnp.concatenate([mine, theirs], axis=1)


def natural_order(values, core):
    mine, theirs = values[:, :HALF], values[:, HALF:]
    even = jnp.where(core == 0, mine, theirs)
    odd = jnp.where(core == 0, theirs, mine)
    pieces = []
    for at in range(0, HALF, 64):
        pieces += [even[:, at : at + 64], odd[:, at : at + 64]]
    return jnp.concatenate(pieces, axis=1)


def normalize(values):
    center = values - jnp.mean(values, axis=-1, keepdims=True)
    spread = jnp.mean(center * center, axis=-1, keepdims=True)
    factor = lax.rsqrt(spread + eps)
    return center * factor, factor


def row(ref, at):
    return ref[at : at + 1, :]


def total(refs, rows=slice(None)):
    result = refs[0][rows, :].astype(jnp.float32)
    for one in refs[1:]:
        result = result + one[rows, :].astype(jnp.float32)
    return result


def enter_grad(place, gout_ref, low_ref, gsum_ref):
    grad = gout_ref[...].astype(jnp.float32)
    gsum_ref[...] = jnp.broadcast_to(jnp.sum(grad, axis=0, keepdims=True), (8, WIDTH))
    low_ref[...] = own_order(grad, place[0]).astype(jnp.bfloat16)


def enter(place, x_ref, vec_ref, resid_ref, low_ref, vecs_ref):
    core = place[0]
    vecs = own_order(vec_ref[...], core)
    vecs_ref[...] = vecs
    resid = own_order(x_ref[:CHUNK, :].astype(jnp.float32), core)
    resid_ref[...] = resid
    scaled, _ = normalize(resid)
    low_ref[:CHUNK, :] = (scaled * vecs[G1 : G1 + 1] + vecs[S1 : S1 + 1]).astype(jnp.bfloat16)
    low_ref[CHUNK:, :] = x_ref[CHUNK:, :]


def add_and_norm(bias_at, gain_at, shift_at):
    def add_norm(place, x_ref, p0, p1, p2, p3, vec_ref, next_ref, low_ref):
        values = x_ref[...] + total((p0, p1, p2, p3)) + row(vec_ref, bias_at)
        next_ref[...] = values
        scaled, _ = normalize(values)
        low_ref[...] = (scaled * row(vec_ref, gain_at) + row(vec_ref, shift_at)).astype(jnp.bfloat16)

    return add_norm


def add_and_leave(bias_at):
    def add_leave(place, x_ref, p0, p1, p2, p3, vec_ref, out_ref):
        values = x_ref[...] + total((p0, p1, p2, p3)) + row(vec_ref, bias_at)
        out_ref[...] = natural_order(values, place[0]).astype(jnp.bfloat16)

    return add_leave


def norm_back(gain_at, last, riders=False):
    def norm_backward(place, x_ref, g_ref, p0, p1, p2, p3, vec_ref, grad_ref, *more):
        core = place[0]
        if riders:
            more[-1][...] = rider_total((p0, p1, p2, p3))
            more = more[:-1]
        d_norm = total((p0, p1, p2, p3), slice(0, CHUNK))
        scaled, factor = normalize(x_ref[...])
        inner = d_norm * row(vec_ref, gain_at)
        mean_one = jnp.mean(inner, axis=-1, keepdims=True)
        mean_two = jnp.mean(inner * scaled, axis=-1, keepdims=True)
        grad = g_ref[...].astype(jnp.float32) + factor * (inner - mean_one - scaled * mean_two)
        low = grad.astype(jnp.bfloat16)
        sums = [
            jnp.sum(d_norm * scaled, axis=0, keepdims=True),
            jnp.sum(d_norm, axis=0, keepdims=True),
            jnp.sum(low.astype(jnp.float32), axis=0, keepdims=True),
            jnp.zeros((5, WIDTH), jnp.float32),
        ]
        if last:
            grad_ref[...] = natural_order(grad, core)
        else:
            grad_ref[...] = grad
            more[0][...] = low
        more[-1][...] = natural_order(jnp.concatenate(sums, axis=0), core)

    return norm_backward


def norm_back_carry(gain_at):
    inner = norm_back(gain_at, False)

    def norm_backward_carry(
        place, x_ref, g_ref, p0, p1, p2, p3, vec_ref, gsum_ref, mid_ref, grad_ref, low_ref, sum_ref
    ):
        inner(place, x_ref, g_ref, p0, p1, p2, p3, vec_ref, grad_ref, low_ref.at[:CHUNK, :], sum_ref)
        rows = [row(gsum_ref, 0), row(mid_ref, 2), sum_ref[0:2, :], mid_ref[0:2, :]]
        rows.append(jnp.zeros((2, WIDTH), jnp.float32))
        ride_along(jnp.concatenate(rows, axis=0), [low_ref])

    return norm_backward_carry


def pack_middle(place, before_ref, mid_ref, out_ref):
    out_ref[0:1, :] = row(before_ref, 2)
    out_ref[1:2, :] = row(mid_ref, 2)
    out_ref[2:4, :] = mid_ref[0:2, :]
    out_ref[4:8, :] = jnp.zeros((4, WIDTH), jnp.float32)


def queries_and_values(ref):
    return jnp.concatenate(
        [ref[0:1, :128], ref[0:1, 384:512], ref[0:1, 256:384], ref[0:1, 640:768]], axis=1
    )


def pack_units(place, sum_ref, up_ref, qkv_ref, out_ref):
    out_ref[...] = sum_ref[...]
    out_ref[6:7, :] = up_ref[0:1, :]
    out_ref[7:8, :HALF] = queries_and_values(qkv_ref)


def pack_riders(place, mid_ref, z0, z1, z2, z3, up_ref, qkv_ref, out_ref):
    late = total((z0, z1, z2, z3))
    rows = [mid_ref[at : at + 1, :] for at in range(4)] + [late[0:1], late[1:2], up_ref[0:1, :]]
    for at, one in enumerate(rows):
        out_ref[2 * at : 2 * at + 1, :] = one[:, :HALF]
        out_ref[2 * at + 1 : 2 * at + 2, :] = one[:, HALF:]
    out_ref[14:15, :] = queries_and_values(qkv_ref)
    out_ref[15:16, :] = jnp.zeros((1, HALF), jnp.float32)


def finish_sums(
    place, early_ref, rider_ref, bout_ref, g1_ref, s1_ref, bdown_ref, g2_ref, s2_ref, bup_ref, bqv_ref
):
    early = early_ref[:8, :] + early_ref[8:, :]
    riders = rider_ref[:16, :] + rider_ref[16:, :]

    def line(at):
        return jnp.concatenate([riders[2 * at : 2 * at + 1], riders[2 * at + 1 : 2 * at + 2]], axis=1)

    def put(ref, first, second):
        ref[0:1, :] = first
        ref[1:2, :] = second

    put(bdown_ref, line(0), early[0:1])
    put(bout_ref, line(1), early[1:2])
    put(g1_ref, line(4), early[2:3])
    put(s1_ref, line(5), early[3:4])
    put(g2_ref, line(2), early[4:5])
    put(s2_ref, line(3), early[5:6])
    first = place[2] == 0
    put(
        bup_ref,
        jnp.where(first, riders[12:13], riders[13:14]),
        jnp.where(first, early[6:7, :HALF], early[6:7, HALF:]),
    )
    for at, sums in enumerate((riders[14:15], early[7:8, :HALF])):
        for kind in range(2):
            pick = jnp.where(
                first,
                sums[:, kind * 256 : kind * 256 + CHUNK],
                sums[:, kind * 256 + CHUNK : kind * 256 + 256],
            )
            bqv_ref[2 * at + kind : 2 * at + kind + 1, :] = pick


def chunk_rows(place, step):
    at = lax.rem(place[1] + step, 4)
    return pl.ds(pl.multiple_of(at * CHUNK, CHUNK), CHUNK)


def assemble(place, pieces, full_ref):
    for piece, step in zip(pieces, AHEAD):
        full_ref[chunk_rows(place, step), :] = piece[:CHUNK, :]


def hand_out(place, part_ref, outs):
    for out, step in zip(outs, AHEAD):
        out[:CHUNK, :] = part_ref[chunk_rows(place, step), :]


def ride_along(rows, outs):
    high = rows.astype(jnp.bfloat16).astype(jnp.float32)
    both = jnp.concatenate([high, rows - high], axis=0).astype(jnp.bfloat16)
    for out in outs:
        out[CHUNK:, :] = both


def rider_total(refs):
    both = total(refs, slice(CHUNK, CHUNK + 16))
    return both[:8] + both[8:]


def qkv_product(place, n0, n1, n2, n3, own_ref, other_ref, bias_ref, full_ref, qkv_ref, kv_ref):
    for piece, step in zip((n0, n1, n2, n3), AHEAD):
        full_ref[chunk_rows(place, step), :] = piece[:CHUNK, :]
    for block in range(2):
        cols = slice(block * 384, block * 384 + 384)
        out = nn_dot(full_ref[:, :HALF], own_ref[block, :, :384])
        out += nn_dot(full_ref[:, HALF:], other_ref[block, :, :384])
        low = (out + bias_ref[0:1, cols]).astype(jnp.bfloat16)
        qkv_ref[:, cols] = low
        kv_ref[:GROUP_ROWS, block * 256 : block * 256 + 256] = low[:, CHUNK:]


def qkv_product_first(
    place, n0, n1, n2, n3, own_ref, other_ref, bias_ref, full_ref, qkv_ref, kv_ref, seg_ref
):
    qkv_product(place, n0, n1, n2, n3, own_ref, other_ref, bias_ref, full_ref, qkv_ref, kv_ref)
    lines = [piece[CHUNK:, :CHUNK] for piece in (n0, n1, n2, n3)]
    for slot in range(4):
        line = lines[0]
        for piece, step in zip(lines[1:], AHEAD[1:]):
            line = jnp.where(lax.rem(place[1] + step, 4) == slot, piece, line)
        line = jnp.where(place[1] == slot, lines[0], line)
        seg_ref[:, slot * CHUNK : (slot + 1) * CHUNK] = line
        kv_ref[GROUP_ROWS:, slot * CHUNK : (slot + 1) * CHUNK] = line


def out_block(ref):
    return jnp.concatenate([ref[0, :, 384:512], ref[1, :, 384:512]], axis=1)


def feed_forward(
    place, n0, n1, n2, n3, own_ref, other_ref, bias_ref, full_ref, pre_ref, act_ref, o0, o1, o2, o3, part_ref
):
    assemble(place, (n0, n1, n2, n3), full_ref)
    for block in range(2):
        cols = slice(block * HALF, (block + 1) * HALF)
        pre = nn_dot(full_ref[:, :HALF], own_ref[block, :, :HALF])
        pre += nn_dot(full_ref[:, HALF:], other_ref[block, :, :HALF])
        pre += bias_ref[0:1, cols]
        pre_ref[:, cols] = pre
        act_ref[:, cols] = jax.nn.gelu(pre, approximate=True).astype(jnp.bfloat16)
    for half, ref in enumerate((own_ref, other_ref)):
        part = nt_dot(act_ref[:, :HALF], ref[0, :, HALF:]) + nt_dot(act_ref[:, HALF:], ref[1, :, HALF:])
        part_ref[:, half * HALF : (half + 1) * HALF] = part.astype(jnp.bfloat16)
    hand_out(place, part_ref, (o0, o1, o2, o3))


def gelu_slope(values):
    scale = 0.7978845608028654
    inner = scale * (values + 0.044715 * values * values * values)
    bend = jnp.tanh(inner)
    return 0.5 * (1.0 + bend) + 0.5 * values * (1.0 - bend * bend) * (
        scale * (1.0 + 3.0 * 0.044715 * values * values)
    )


def feed_backward(
    place, n0, n1, n2, n3, own_ref, other_ref, pre_ref, full_ref, dpre_ref, sum_ref, o0, o1, o2, o3, part_ref
):
    assemble(place, (n0, n1, n2, n3), full_ref)
    for block in range(2):
        cols = slice(block * HALF, (block + 1) * HALF)
        d_act = nn_dot(full_ref[:, :HALF], own_ref[block, :, HALF:])
        d_act += nn_dot(full_ref[:, HALF:], other_ref[block, :, HALF:])
        d_pre = (d_act * gelu_slope(pre_ref[:, cols])).astype(jnp.bfloat16)
        dpre_ref[:, cols] = d_pre
        sum_ref[0:1, cols] = jnp.sum(d_pre.astype(jnp.float32), axis=0, keepdims=True)
    for half, ref in enumerate((own_ref, other_ref)):
        part = nt_dot(dpre_ref[:, :HALF], ref[0, :, :HALF]) + nt_dot(dpre_ref[:, HALF:], ref[1, :, :HALF])
        part_ref[:, half * HALF : (half + 1) * HALF] = part.astype(jnp.bfloat16)
    hand_out(place, part_ref, (o0, o1, o2, o3))


def feed_backward_riders(place, *refs):
    feed_backward(place, *refs[:-2], refs[-1])
    refs[-2][...] = rider_total(refs[:4])


def qkv_backward_riders(place, rider_ref, *refs):
    qkv_backward(place, *refs)
    ride_along(rider_ref[...], refs[-5:-1])


def feed_weight_grads(place, norm_ref, dpre_ref, grad_ref, act_ref, keep_ref, give_ref, done_ref):
    done_ref[...] = jnp.zeros_like(done_ref)
    for first, left, right in ((0, norm_ref, dpre_ref), (HALF, grad_ref, act_ref)):
        for half, out in enumerate((keep_ref, give_ref)):
            left_t = left[:, half * HALF : (half + 1) * HALF].T
            for block in range(2):
                product = nn_dot(left_t, right[:, block * HALF : (block + 1) * HALF])
                out[block, :, first : first + HALF] = product.astype(jnp.bfloat16)


def attn_weight_grads(place, norm_ref, dqkv_ref, grad_ref, mixed_ref, keep_ref, give_ref, done_ref):
    done_ref[...] = jnp.zeros_like(done_ref)
    for half, out in enumerate((keep_ref, give_ref)):
        rows = slice(half * HALF, (half + 1) * HALF)
        norm_t = norm_ref[:, rows].T
        grad_t = grad_ref[:, rows].T
        outer = nn_dot(grad_t, mixed_ref[...]).astype(jnp.bfloat16)
        for block in range(2):
            product = nn_dot(norm_t, dqkv_ref[:, block * 384 : block * 384 + 384])
            out[block, :, :384] = product.astype(jnp.bfloat16)
            out[block, :, 384:] = outer[:, block * CHUNK : (block + 1) * CHUNK]


def mix_gradient(place, n0, n1, n2, n3, own_ref, other_ref, full_ref, dmix_ref):
    assemble(place, (n0, n1, n2, n3), full_ref)
    d_mix = nn_dot(full_ref[:, :HALF], out_block(own_ref)) + nn_dot(
        full_ref[:, HALF:], out_block(other_ref)
    )
    dmix_ref[...] = d_mix.astype(jnp.bfloat16)


def qkv_backward(
    place, dq_ref, mine_ref, came_ref, own_ref, other_ref, dqkv_ref, sum_ref, o0, o1, o2, o3, part_ref
):
    d_kv = (mine_ref[...] + came_ref[...].astype(jnp.float32)).astype(jnp.bfloat16)
    for block in range(2):
        base = block * 384
        dqkv_ref[:, base : base + CHUNK] = dq_ref[:, block * CHUNK : (block + 1) * CHUNK]
        dqkv_ref[:, base + CHUNK : base + 384] = d_kv[:, block * 256 : block * 256 + 256]
    sum_ref[0:1, :] = jnp.sum(dqkv_ref[...].astype(jnp.float32), axis=0, keepdims=True)
    for half, ref in enumerate((own_ref, other_ref)):
        part = nt_dot(dqkv_ref[:, :384], ref[0, :, :384]) + nt_dot(dqkv_ref[:, 384:], ref[1, :, :384])
        part_ref[:, half * HALF : (half + 1) * HALF] = part.astype(jnp.bfloat16)
    hand_out(place, part_ref, (o0, o1, o2, o3))


def interleave(own, other):
    pieces = []
    for at in range(own.shape[0] // CHUNK):
        pieces += [own[at * CHUNK : (at + 1) * CHUNK], other[at * CHUNK : (at + 1) * CHUNK]]
    return jnp.concatenate(pieces, axis=0)


def by_head(block):
    first = lax.broadcasted_iota(jnp.int32, block.shape, 1) < HEAD_DIM
    zero = jnp.zeros_like(block)
    return jnp.concatenate([jnp.where(first, block, zero), jnp.where(first, zero, block)], axis=0)


def pick_heads(both):
    first = lax.broadcasted_iota(jnp.int32, (CHUNK, CHUNK), 0) < HEAD_DIM
    return jnp.where(first, both[:, :CHUNK], both[:, CHUNK:]).T


def tile_masks(place, own_ref, other_ref):
    down = lax.broadcasted_iota(jnp.int32, (CHUNK, CHUNK), 0)
    across = lax.broadcasted_iota(jnp.int32, (CHUNK, CHUNK), 1)
    tiles = GROUP_ROWS // CHUNK

    def line(ref, at):
        return ref[0:1, at * CHUNK : (at + 1) * CHUNK].astype(jnp.float32)

    def column(ref, at):
        return jnp.broadcast_to(line(ref, at), (CHUNK, CHUNK)).T

    own = [column(own_ref, at) for at in range(tiles)]
    other = [column(other_ref, at) for at in range(tiles)]
    masks = []
    for at in range(tiles):
        rows = line(own_ref, at)
        used = rows >= 0.0
        blocks = []
        for key_at in range(at + 1):
            from_own = (own[key_at] == rows) & used
            from_other = (other[key_at] == rows) & used
            if key_at == at:
                from_own = (from_own & (down <= across)) | (down == across)
                from_other = from_other & (place[0] == 1)
            blocks += [jnp.where(from_own, 0.0, big_negative), jnp.where(from_other, 0.0, big_negative)]
        mask = jnp.concatenate(blocks, axis=0)
        masks.append(jnp.concatenate([mask, mask], axis=1))
    return masks


def masked_scores(keys_all, q_heads, bias):
    scores = nt_dot(keys_all, q_heads) * score_scale
    return jnp.where(bias < 0.0, big_negative, scores)


def kv_blocks(qkv_ref, kv_ref, block):
    base = block * 3 * CHUNK
    k_own = qkv_ref[:, base + CHUNK : base + 2 * CHUNK]
    v_own = qkv_ref[:, base + 2 * CHUNK : base + 3 * CHUNK]
    k_other = kv_ref[:GROUP_ROWS, block * 2 * CHUNK : block * 2 * CHUNK + CHUNK]
    v_other = kv_ref[:GROUP_ROWS, block * 2 * CHUNK + CHUNK : block * 2 * CHUNK + 2 * CHUNK]
    return interleave(k_own, k_other), interleave(v_own, v_other)


def attend_forward(
    place, qkv_ref, kv_ref, seg_ref, seg_other_ref, own_ref, other_ref, mixed_ref, lse_ref, o0, o1, o2, o3, part_ref
):
    tiles = GROUP_ROWS // CHUNK
    biases = tile_masks(place, seg_ref, seg_other_ref)
    for block in range(2):
        base = block * 3 * CHUNK
        keys_all, values_all = kv_blocks(qkv_ref, kv_ref, block)
        values_t = values_all.T
        for at in range(tiles):
            rows = slice(at * CHUNK, (at + 1) * CHUNK)
            count = 2 * CHUNK * (at + 1)
            q_heads = by_head(qkv_ref[rows, base : base + CHUNK])
            scores = masked_scores(keys_all[:count], q_heads, biases[at])
            top = jnp.max(scores, axis=0, keepdims=True)
            expo = jnp.exp(scores - top)
            weight = jnp.sum(expo, axis=0, keepdims=True)
            prob = (expo * (1.0 / weight)).astype(jnp.bfloat16)
            mixed = pick_heads(nn_dot(values_t[:, :count], prob))
            mixed_ref[rows, block * CHUNK : (block + 1) * CHUNK] = mixed.astype(jnp.bfloat16)
            lse = top + jnp.log(weight)
            lse_ref[2 * block : 2 * block + 1, rows] = lse[:, :CHUNK]
            lse_ref[2 * block + 1 : 2 * block + 2, rows] = lse[:, CHUNK:]
    for half, ref in enumerate((own_ref, other_ref)):
        part = nt_dot(mixed_ref[...], out_block(ref))
        part_ref[:, half * HALF : (half + 1) * HALF] = part.astype(jnp.bfloat16)
    hand_out(place, part_ref, (o0, o1, o2, o3))


def attend_backward(
    place, qkv_ref, kv_ref, seg_ref, seg_other_ref, lse_ref, dmix_ref, dq_ref, own_ref, other_ref, dk_ref, dv_ref
):
    tiles = GROUP_ROWS // CHUNK
    biases = tile_masks(place, seg_ref, seg_other_ref)
    for block in range(2):
        base = block * 3 * CHUNK
        keys_all, values_all = kv_blocks(qkv_ref, kv_ref, block)
        keys_t = keys_all.T
        for at in reversed(range(tiles)):
            rows = slice(at * CHUNK, (at + 1) * CHUNK)
            count = 2 * CHUNK * (at + 1)
            q_heads = by_head(qkv_ref[rows, base : base + CHUNK])
            dm_heads = by_head(dmix_ref[rows, block * CHUNK : (block + 1) * CHUNK])
            lse = jnp.concatenate(
                [lse_ref[2 * block : 2 * block + 1, rows], lse_ref[2 * block + 1 : 2 * block + 2, rows]],
                axis=1,
            )
            scores = masked_scores(keys_all[:count], q_heads, biases[at])
            prob = jnp.exp(scores - lse)
            dprob = nt_dot(values_all[:count], dm_heads)
            weighted = jnp.sum(prob * dprob, axis=0, keepdims=True)
            dscore = (prob * (dprob - weighted)).astype(jnp.bfloat16)
            prob_low = prob.astype(jnp.bfloat16)
            dq = pick_heads(nn_dot(keys_t[:, :count], dscore)) * score_scale
            dq_ref[rows, block * CHUNK : (block + 1) * CHUNK] = dq.astype(jnp.bfloat16)
            dk = nn_dot(dscore, q_heads) * score_scale
            dv = nn_dot(prob_low, dm_heads)
            if at == tiles - 1:
                dk_ref[...] = dk
                dv_ref[...] = dv
            else:
                dk_ref[:count] += dk
                dv_ref[:count] += dv
        for at in range(tiles):
            rows = slice(at * CHUNK, (at + 1) * CHUNK)
            mine = slice(2 * at * CHUNK, (2 * at + 1) * CHUNK)
            theirs = slice((2 * at + 1) * CHUNK, (2 * at + 2) * CHUNK)
            k_cols = slice(block * 2 * CHUNK, block * 2 * CHUNK + CHUNK)
            v_cols = slice(block * 2 * CHUNK + CHUNK, block * 2 * CHUNK + 2 * CHUNK)
            own_ref[rows, k_cols] = dk_ref[mine]
            own_ref[rows, v_cols] = dv_ref[mine]
            other_ref[rows, k_cols] = dk_ref[theirs].astype(jnp.bfloat16)
            other_ref[rows, v_cols] = dv_ref[theirs].astype(jnp.bfloat16)


def local(
    hidden_in,
    segment_ids,
    w_qkv,
    b_qv,
    w_out,
    b_out,
    ln1_gain,
    ln1_bias,
    w_up,
    b_up,
    w_down,
    b_down,
    ln2_gain,
    ln2_bias,
    out_grad,
):
    layer_count = w_qkv.shape[0]
    core = lax.axis_index("c")
    lane = lax.axis_index("xl")
    place = jnp.stack([core, lax.axis_index("z"), lane]).astype(jnp.int32)

    ids = segment_ids.astype(jnp.bfloat16).reshape(1, CHUNK)
    ids = jnp.pad(ids, ((0, 15), (0, WIDTH - CHUNK)))
    moved = swap_rows(jnp.concatenate([hidden_in, ids], axis=0))
    moved_grad = swap_rows(out_grad)
    vec_rows = []
    for at in range(layer_count):
        vec_rows += [b_down[at], b_out[at], ln1_gain[at], ln1_bias[at], ln2_gain[at], ln2_bias[at]]
    vecs = jnp.concatenate([jnp.stack(vec_rows), jnp.zeros((4, WIDTH), jnp.float32)], axis=0)

    attn_slab = [
        jnp.concatenate([w_qkv[at].reshape(64, 3 * CHUNK), w_out[at].T], axis=1)
        for at in range(layer_count)
    ]
    feed_slab = [jnp.concatenate([w_up[at], w_down[at].T], axis=1) for at in range(layer_count)]
    attn_own = [share(attn_slab[0], PLANE, 16).reshape(2, HALF, 512)]

    resid, normed, vecs = call(
        enter,
        [place, moved, vecs],
        [fl(CHUNK, WIDTH), bf(CHUNK + 16, WIDTH), fl(16, WIDTH)],
        vmem=6,
    )
    bias_mine = jnp.concatenate([b_qv.reshape(layer_count, 2 * CHUNK), b_up], axis=1)
    bias_next = lax.ppermute(bias_mine, "xl", [(0, 1), (1, 0)])
    bias_both = jnp.stack(
        [jnp.where(lane == 0, bias_mine, bias_next), jnp.where(lane == 0, bias_next, bias_mine)], axis=1
    )

    pieces = gather_z(normed)
    pieces, (bias_both, moved_grad) = tie(pieces, (bias_both, moved_grad))
    attn_w = [(attn_own[0], other_core(attn_own[0]))]
    feed_w = []
    attn_own.append(share(attn_slab[1], PLANE, 16).reshape(2, HALF, 512))
    feed_own = [None, share(feed_slab[1], PLANE, 16).reshape(2, HALF, 1024)]
    grad, grad_sum = call(enter_grad, [place, moved_grad], [bf(CHUNK, WIDTH), fl(8, WIDTH)], vmem=6)
    lows = gather_z(grad)

    part_scratch = [pltpu.VMEM((GROUP_ROWS, WIDTH), jnp.bfloat16)]
    full = bf(GROUP_ROWS, WIDTH)
    piece = bf(CHUNK, WIDTH)

    saved = []
    for at in range(layer_count):
        base = 6 * at
        zero = jnp.zeros((2, CHUNK), jnp.float32)
        qkv_bias = jnp.concatenate(
            [bias_both[at][:, :CHUNK], zero, bias_both[at][:, CHUNK : 2 * CHUNK]], axis=1
        ).reshape(1, 6 * CHUNK)
        up_bias = bias_both[at][:, 2 * CHUNK :].reshape(1, 1024)
        first = at == 0
        here = place
        if first:
            here, grad = tie(place, grad)
        normed_full, qkv, kv_mine, *ids = call(
            qkv_product_first if first else qkv_product,
            [here, *pieces, *attn_w[at], qkv_bias],
            [full, bf(GROUP_ROWS, 768), bf(GROUP_ROWS + 16 * first, 512)] + [bf(16, 512)] * first,
            flops=2200000000,
            vmem=11,
        )
        kv_other = other_core(kv_mine)
        if first:
            segs, segs_other = ids[0], kv_other[GROUP_ROWS:]
            feed_slab[0], (segs, lows) = tie(feed_slab[0], (segs, lows))
            feed_own[0] = share(feed_slab[0], PLANE, 16).reshape(2, HALF, 1024)
        here = place
        if not first:
            here, feed_own[1] = tie(place, feed_own[1])
        mixed, lse, *parts = call(
            attend_forward,
            [here, qkv, kv_other, segs, segs_other, *attn_w[at]],
            [bf(GROUP_ROWS, 256), fl(8, GROUP_ROWS), piece, piece, piece, piece],
            part_scratch,
            flops=6300000000,
            vmem=16,
        )
        resid_mid, cnorm = call(
            add_and_norm(base + BOUT, base + G2, base + S2),
            [place, resid, *scatter_z(parts), vecs],
            [fl(CHUNK, WIDTH), piece],
            vmem=6,
        )
        cnorm, feed_own[at] = tie(cnorm, feed_own[at])
        feed_w.append((feed_own[at], other_core(feed_own[at])))
        cnorm_full, pre_up, act, *parts = call(
            feed_forward,
            [place, *gather_z(cnorm), *feed_w[at], up_bias],
            [full, fl(GROUP_ROWS, WIDTH), full, piece, piece, piece, piece],
            part_scratch,
            flops=5200000000,
            vmem=18,
        )
        saved.append((resid, normed_full, qkv, kv_other, mixed, lse, resid_mid, cnorm_full, pre_up, act))
        parts = scatter_z(parts)
        if at < layer_count - 1:
            resid, normed = call(
                add_and_norm(base + BDOWN, base + 6 + G1, base + 6 + S1),
                [place, resid_mid, *parts, vecs],
                [fl(CHUNK, WIDTH), piece],
                vmem=6,
            )
            normed, attn_own[1] = tie(normed, attn_own[1])
            attn_w.append((attn_own[1], other_core(attn_own[1])))
            pieces = gather_z(normed)
    last_parts = parts

    attn_out = [None] * layer_count
    feed_out = [None] * layer_count
    for at in reversed(range(layer_count)):
        base = 6 * at
        resid_in, normed_full, qkv, kv_other, mixed, lse, resid_mid, cnorm_full, pre_up, act = saved[at]

        top = at == layer_count - 1
        sent = piece if top else bf(CHUNK + 16, WIDTH)
        here = place
        if not top:
            here, feed_came = tie(place, feed_came)
            feed_out[1] = jnp.sum(feed_came.astype(jnp.float32), axis=0)
        low_full, d_pre, bup_sum, *parts = call(
            feed_backward if top else feed_backward_riders,
            [here, *lows, *feed_w[at], pre_up],
            [full, full, fl(1, WIDTH), piece, piece, piece, piece] + [fl(8, WIDTH)] * (not top),
            part_scratch,
            flops=5800000000,
            vmem=18,
        )
        early_sum = parts[4:]
        arrived = scatter_z(parts[:4])
        here = place
        if top:
            here, last_parts = tie(place, last_parts)
        keep, give, done = call(
            feed_weight_grads,
            [here, cnorm_full, d_pre, low_full, act],
            [bf(2, HALF, 1024), bf(2, HALF, 1024), fl(8, CHUNK)],
            flops=3500000000,
            vmem=18,
        )
        feed_sum = (keep.astype(jnp.float32) + other_core(give).astype(jnp.float32)).astype(jnp.bfloat16)
        arrived, done = tie(arrived, done)
        grad, low, mid_sums = call(
            norm_back(base + G2, False),
            [place, resid_mid, grad, *arrived, vecs],
            [fl(CHUNK, WIDTH), piece, fl(8, WIDTH)],
            vmem=6,
            after=[done],
        )

        middle = gather_z(low)
        mix_here, feed_sum = tie(place, feed_sum)
        if not top:
            mix_here, attn_came = tie(mix_here, attn_came)
            attn_out[1] = jnp.sum(attn_came.astype(jnp.float32), axis=0)
        if at == 0:
            (riders,) = call(pack_middle, [place, sums, mid_sums], [fl(8, WIDTH)], vmem=4)
            (early,) = call(
                pack_units, [place, early_sum[0], *before], [fl(8, WIDTH)], vmem=4
            )
            early = early + other_core(early)
            high = early.astype(jnp.bfloat16)
            rest = (early - high.astype(jnp.float32)).astype(jnp.bfloat16)
            early = jnp.broadcast_to(jnp.concatenate([high, rest])[None], (16, 16, WIDTH))
            payload = jnp.concatenate([feed_sum.reshape(16, 64, 1024), early], axis=1)
            feed_came = lax.all_to_all(payload, PLANE, 0, 0, tiled=True)
        else:
            feed_came = lax.all_to_all(feed_sum.reshape(16, 64, 1024), PLANE, 0, 0, tiled=True)
        low_full, d_mix = call(
            mix_gradient,
            [mix_here, *middle, *attn_w[at]],
            [full, bf(GROUP_ROWS, 256)],
            flops=1200000000,
            vmem=8,
        )
        d_q, d_own, d_other = call(
            attend_backward,
            [place, qkv, kv_other, segs, segs_other, lse, d_mix],
            [bf(GROUP_ROWS, 256), fl(GROUP_ROWS, 512), bf(GROUP_ROWS, 512)],
            [pltpu.VMEM((2 * GROUP_ROWS, CHUNK), jnp.float32)] * 2,
            flops=7700000000,
            vmem=16,
        )
        d_qkv, bqkv_sum, *parts = call(
            qkv_backward if top else qkv_backward_riders,
            [place, *(() if top else (riders,)), d_q, d_own, other_core(d_other), *attn_w[at]],
            [bf(GROUP_ROWS, 768), fl(1, 768), sent, sent, sent, sent],
            part_scratch,
            flops=2300000000,
            vmem=11,
        )
        if top:
            (hidden,) = call(
                add_and_leave(base + BDOWN), [place, resid_mid, *last_parts, vecs], [piece], vmem=6
            )
            hidden_out = swap_rows(hidden)
        arrived = scatter_z(parts)
        keep, give, done = call(
            attn_weight_grads,
            [place, normed_full, d_qkv, low_full, mixed],
            [bf(2, HALF, 512), bf(2, HALF, 512), fl(8, CHUNK)],
            flops=2600000000,
            vmem=11,
        )
        attn_sum = (keep.astype(jnp.float32) + other_core(give).astype(jnp.float32)).astype(jnp.bfloat16)
        arrived, done = tie(arrived, done)
        here, hidden_out = tie(place, hidden_out)
        if top:
            grad, low, sums = call(
                norm_back_carry(base + G1),
                [here, resid_in, grad, *arrived, vecs, grad_sum, mid_sums],
                [fl(CHUNK, WIDTH), bf(CHUNK + 16, WIDTH), fl(8, WIDTH)],
                vmem=7,
                after=[done],
            )
        else:
            here, feed_came = tie(here, feed_came)
            came = jnp.sum(feed_came.astype(jnp.float32), axis=0)
            feed_out[0], early = came[:64], came[64:]
            grad, sums, riders = call(
                norm_back(base + G1, True, True),
                [here, resid_in, grad, *arrived, vecs],
                [fl(CHUNK, WIDTH), fl(8, WIDTH), fl(8, WIDTH)],
                vmem=6,
                after=[done],
            )

        if at > 0:
            attn_came = lax.all_to_all(attn_sum.reshape(16, 64, 512), PLANE, 0, 0, tiled=True)
            lows = gather_z(low)
            before = [bup_sum, bqkv_sum]
        else:
            late = gather_z(sums)
            (riders,) = call(
                pack_riders, [place, riders, *late, bup_sum, bqkv_sum], [fl(16, HALF)], vmem=4
            )
            riders = riders + other_core(riders)
            high = riders.astype(jnp.bfloat16)
            rest = (riders - high.astype(jnp.float32)).astype(jnp.bfloat16)
            riders = jnp.broadcast_to(jnp.concatenate([high, rest])[None], (16, 32, HALF))
            payload = jnp.concatenate([attn_sum.reshape(16, 64, 512), riders], axis=1)
            hidden_grad, payload = tie(swap_rows(grad), payload)
            came = lax.all_to_all(payload, PLANE, 0, 0, tiled=True)
            came = jnp.sum(came.astype(jnp.float32), axis=0)
            attn_out[0], riders = came[:64], came[64:]

    sum_bout, sum_g1, sum_s1, sum_bdown, sum_g2, sum_s2, sum_bup, sum_bqv = call(
        finish_sums,
        [place, early, riders],
        [fl(2, WIDTH)] * 6 + [fl(2, 512), fl(4, CHUNK)],
        vmem=6,
    )
    sum_bqv = sum_bqv.reshape(2, 2, CHUNK)

    grad_w_qkv = jnp.stack([attn_out[at][:, :384].reshape(64, 3, CHUNK) for at in range(layer_count)])
    grad_w_out = jnp.stack([attn_out[at][:, 384:].T for at in range(layer_count)])
    grad_w_up = jnp.stack([feed_out[at][:, :512] for at in range(layer_count)])
    grad_w_down = jnp.stack([feed_out[at][:, 512:].T for at in range(layer_count)])
    return (
        hidden_out,
        hidden_grad,
        grad_w_qkv,
        sum_bqv,
        grad_w_out,
        sum_bout,
        sum_g1,
        sum_s1,
        grad_w_up,
        sum_bup,
        grad_w_down,
        sum_bdown,
        sum_g2,
        sum_s2,
    )


def solution(mesh):
    inner = Mesh(mesh.devices.reshape(2, 4, 2, 4, 2), AXES)
    dp = ("xh", "y", "c")
    tensor = ("z", "xl")
    rows = dp + tensor
    in_specs = (
        P(rows, None),
        P(rows),
        P(None, dp, None, tensor),
        P(None, None, tensor),
        P(None, tensor, dp),
        P(),
        P(),
        P(),
        P(None, dp, tensor),
        P(None, tensor),
        P(None, tensor, dp),
        P(),
        P(),
        P(),
        P(rows, None),
    )
    out_specs = (
        P(rows, None),
        P(rows, None),
        P(None, dp, None, tensor),
        P(None, None, tensor),
        P(None, tensor, dp),
        P(),
        P(),
        P(),
        P(None, dp, tensor),
        P(None, tensor),
        P(None, tensor, dp),
        P(),
        P(),
        P(),
    )
    return jax.shard_map(local, mesh=inner, in_specs=in_specs, out_specs=out_specs, check_vma=False)
```
